32 devices in a mesh: inv: 2 (over y), rcp: 4 (over z), reg: 2 (over x), tm: 2 (over core).
Axes of the slice: x: 2, y: 2, z: 4, core: 2. Of those that a mesh axis runs over, the one named last changes fastest.
Arguments:
- probes: bfloat16 [1024, 8, 2048], P(('inv', 'rcp')), parts along dimension 0, may hold values from -6 to 6
- footprint: bfloat16 [256, 16, 4, 256], P(('inv', 'rcp', 'reg'), None, 'tm'), parts along dimension 0, may hold values from 0.0029907227 to 0.099609375
- blocks: int32 [256, 16], P(('inv', 'rcp', 'reg')), parts along dimension 0, may hold values from 0 to 511, as said below
- hour_start: int32 [256], P(('inv', 'rcp', 'reg')), parts along dimension 0, may hold values from 0 to 4
- obs_weight: float32 [256], P(('inv', 'rcp', 'reg')), parts along dimension 0, may hold values from 0.5 to 4
- placement: int32 [1024], P('inv'), parts along dimension 0, may hold values from 0 to 511, as said below
Outputs:
- hessian_probe: float32 [1024, 8, 2048], P(('inv', 'rcp'), None, ('reg', 'tm')), parts along dimension 0
The draws below stay inside these ranges and needn't reach their ends.
There are 2 independent parts, one for each index of `inv`. The reference program is written for one: setup_inputs(seed, part) draws one part's arguments, and reference() takes and returns one part's arrays. A program takes and returns all parts, laid end to end along the dimension named above; each array names one. Nothing has to cross between parts.
Inputs may be any that keep to these rules, and one draw needn't show every extreme that they name: Rows come in aligned blocks of 16 receptors, block d belonging to region group d % 2. Among the 256 entries of one block, at most 96 have placement[blocks] // 128 equal to any one value; in every region group one such value is taken exactly 96 times by every block of the group. Blocks may repeat. `placement`: A permutation of the 512 block rows.
All inputs are finite; a program needn't handle non-finite values.
Results may differ from the reference program's by a relative error of at most 0.0003.
Values may be sent and summed in bfloat16 or wider, within the bound.
No kernel may reach another device: no remote copies, remote signals or barrier semaphores. Data moves between devices by JAX's collectives and lax.ppermute only.
A program may use at most 64 MiB of HBM per device.

```python
import math
import jax
import jax.numpy as jnp
from jax import lax

K = 8
CELLS = 256
BLK_DEV = 128
HOURS = 8
WIN = 4
RCP_DEV = 16
SLOTS = 16
OWNERS = 4
REGIONS = 2
CAP = 96
NBLK = 512
RECEPTORS = 128


def layout(key):
    devices = OWNERS * REGIONS
    entries = RCP_DEV * SLOTS
    remaining = entries - CAP
    key_hot, key_order, key_shuffle, key_local, key_perm = jax.random.split(jax.random.fold_in(key, 11), 5)
    hottest = jax.random.randint(key_hot, (REGIONS,), 0, OWNERS)
    device_hot = hottest[jnp.arange(devices) % REGIONS]
    others = jax.vmap(lambda subkey: jax.random.permutation(subkey, OWNERS - 1))(jax.random.split(key_order, devices))
    position = jnp.arange(entries)
    stride = jnp.clip((position - CAP) * (OWNERS - 1) // remaining, 0, OWNERS - 2)
    picked_other = jnp.take_along_axis(others, jnp.broadcast_to(stride[None, :], (devices, entries)), axis=1)
    other_owner = (device_hot[:, None] + 1 + picked_other) % OWNERS
    owner_of = jnp.where(position[None, :] < CAP, device_hot[:, None], other_owner)
    shuffle = jax.vmap(lambda subkey: jax.random.permutation(subkey, entries))(jax.random.split(key_shuffle, devices))
    owner_of = jnp.take_along_axis(owner_of, shuffle, axis=1)
    local_row = jax.random.randint(key_local, (devices, entries), 0, BLK_DEV)
    stored = owner_of * BLK_DEV + local_row
    first_entry = stored[0, 0]
    ordering = jax.random.permutation(key_perm, NBLK)
    where_first = jnp.argmax(ordering == first_entry)
    last_value = ordering[NBLK - 1]
    ordering = ordering.at[where_first].set(last_value).at[NBLK - 1].set(first_entry)
    inverse = jnp.zeros((NBLK,), jnp.int32).at[ordering].set(jnp.arange(NBLK, dtype=jnp.int32))
    geographic = inverse[stored].reshape(devices * RCP_DEV, SLOTS)
    return (ordering.astype(jnp.int32), geographic.astype(jnp.int32))


def draw_placement(key, part):
    shared = layout(key)
    return shared[0]


def draw_blocks(key, part):
    shared = layout(key)
    return shared[1]


def set_ends(values, own_key, low, largest):
    extent = values.shape
    spot = [jax.random.randint(jax.random.fold_in(own_key, axis), (), 0, extent[axis]) for axis in range(len(extent))]
    values = values.at[tuple(spot)].set(low)
    longest = extent.index(max(extent))
    spot[longest] = (spot[longest] + 1) % extent[longest]
    return values.at[tuple(spot)].set(largest)


def levels(own_key, shape, pieces, least, top_value):
    def one(axis_at, parts):
        draws = jax.random.uniform(jax.random.fold_in(jax.random.fold_in(own_key, 6), axis_at), (parts,), jnp.float32, least / len(pieces), top_value / len(pieces))
        return jnp.repeat(jnp.exp(draws), shape[axis_at] // parts).reshape((-1,) + (1,) * (len(shape) - axis_at - 1))

    gain = one(*pieces[0])
    for cut in pieces[1:]:
        gain = gain * one(*cut)
    return gain


def centred(key, dims, scale, reach, cuts=(), kind=jnp.bfloat16):
    level = levels(key, dims, cuts, -0.22, 0.18) if cuts else 1.0
    drawn = jax.random.normal(key, dims, jnp.float32) * scale * level
    return jnp.minimum(jnp.maximum(drawn, -reach), reach).astype(kind)


def setup_inputs(seed: int = 0, part: int = 0) -> dict:
    key_list = jax.random.split(jax.random.key(seed), 7)
    part_splits = jax.random.split(jax.random.fold_in(key_list[6], part), 7)
    return {
        "probes": centred(part_splits[0], (NBLK, HOURS, K * CELLS), 1.0, 6.0, ((0, 4),)),
        "footprint": jnp.clip(jnp.exp(math.log(0.099609375) - 3.5057412 * jax.random.uniform(part_splits[1], (RECEPTORS, SLOTS, WIN, CELLS), jnp.float32) ** levels(part_splits[1], (RECEPTORS, SLOTS, WIN, CELLS), ((0, 8), (2, 2)), -0.2, 0.2)), 0.0029907227, 0.099609375).astype(jnp.bfloat16),
        "blocks": draw_blocks(jax.random.fold_in(jax.random.fold_in(key_list[6], part), 71), part),
        "hour_start": set_ends(jax.random.randint(part_splits[3], (RECEPTORS,), 0, HOURS - WIN + 1), jax.random.fold_in(part_splits[3], 1), 0, HOURS - WIN).astype(jnp.int32),
        "obs_weight": jnp.clip(jnp.exp(math.log(4.0) - 2.0794415 * jax.random.uniform(part_splits[4], (RECEPTORS,), jnp.float32) ** levels(part_splits[4], (RECEPTORS,), ((0, 8),), -0.2, 0.2)), 0.5, 4.0),
        "placement": draw_placement(jax.random.fold_in(jax.random.fold_in(key_list[6], part), 71), part),
    }


def reference(probes, footprint, blocks, hour_start, obs_weight, placement):
    stored = placement[blocks]
    flat_rows = probes.reshape(NBLK * HOURS, K, CELLS)
    hours_ahead = jnp.arange(WIN, dtype=jnp.int32)
    group_count = RECEPTORS // RCP_DEV

    def one_group(summed, group_index):
        first_row = group_index * RCP_DEV
        group_rows = lax.dynamic_slice_in_dim(stored, first_row, RCP_DEV, 0)
        group_start = lax.dynamic_slice_in_dim(hour_start, first_row, RCP_DEV, 0)
        group_print = lax.dynamic_slice_in_dim(footprint, first_row, RCP_DEV, 0).astype(jnp.float32)
        group_weight = lax.dynamic_slice_in_dim(obs_weight, first_row, RCP_DEV, 0)
        row_index = group_rows[:, :, None] * HOURS + group_start[:, None, None] + hours_ahead[None, None, :]
        probe_rows = flat_rows[row_index].astype(jnp.float32)
        observed = jnp.einsum("rswc,rswkc->rk", group_print, probe_rows, precision=lax.Precision.HIGHEST)
        weighted = group_weight[:, None] * observed
        entry_terms = group_print[:, :, :, None, :] * weighted[:, None, None, :, None]
        summed = summed.at[row_index.reshape(-1)].add(entry_terms.reshape(-1, K, CELLS))
        return summed, None

    start_sum = jnp.zeros((NBLK * HOURS, K, CELLS), jnp.float32)
    summed, unused = lax.scan(one_group, start_sum, jnp.arange(group_count, dtype=jnp.int32))
    return summed.reshape(NBLK, HOURS, K * CELLS)
```

```python
import functools

import jax
import jax.numpy as jnp
from jax import lax
from jax.experimental import pallas as pl
from jax.experimental.pallas import tpu as pltpu
from jax.sharding import PartitionSpec as P

F32 = jnp.float32
BF16 = jnp.bfloat16
I32 = jnp.int32
META = 16
VMEM_LIMIT = 48 * 1024 * 1024


def up(x, m):
    return (x + m - 1) // m * m


def log2(x):
    assert x & (x - 1) == 0
    return x.bit_length() - 1


def iota(shape, axis):
    return lax.broadcasted_iota(I32, shape, axis)


def mask(cond):
    return jnp.where(cond, jnp.float32(1), jnp.float32(0))


def nt(a, b):
    return lax.dot_general(a, b, (((1,), (1,)), ((), ())), preferred_element_type=F32)


def nn(a, b):
    return lax.dot_general(a, b, (((1,), (0,)), ((), ())), preferred_element_type=F32)


def pack_kernel(cfg, where_ref, blocks_ref, hour_ref, weight_ref, place_ref, fp_ref, *outs):
    n, capp, local_blocks, slots, w2 = cfg["n"], cfg["capp"], cfg["local"], cfg["slots"], cfg["w2"]
    receptors = blocks_ref.shape[0]
    cols = receptors * slots * w2
    ids = place_ref.shape[1]
    used = n * capp
    padded = up(used, 256)
    me = where_ref[0]
    tm = where_ref[1]
    lane = iota((1, cols), 1)
    entry = lane >> log2(w2)
    w_of = lane & (w2 - 1)
    s_of = entry & (slots - 1)
    r_of = entry >> log2(slots)
    b = blocks_ref[...]
    sel_s = mask(iota((slots, cols), 0) == s_of).astype(BF16)
    high = (b >> 6).astype(F32).astype(BF16)
    low = (b & 63).astype(F32).astype(BF16)
    spread = nn(high, sel_s) * 64.0 + nn(low, sel_s)
    on_row = iota((receptors, cols), 0) == r_of
    geo = jnp.sum(jnp.where(on_row, spread, 0.0), axis=0, keepdims=True).astype(I32)
    place = place_ref[...]
    row16 = iota((16, ids), 0)
    owner_tab = (place >> log2(local_blocks)).astype(F32)
    local_tab = (place & (local_blocks - 1)).astype(F32)
    tab = jnp.where(row16 == 0, owner_tab, jnp.where(row16 == 1, local_tab, 0.0)).astype(BF16)
    found = nn(tab, mask(iota((ids, cols), 0) == geo).astype(BF16))
    step = found[0:1].astype(I32) - me
    step = jnp.where(step < 0, step + n, step)
    local_row = found[1:2]
    nr = up(n, 16)
    to_owner = iota((nr, cols), 0) == step
    before = ((iota((cols, cols), 0) >> log2(w2)) < entry) & ((iota((cols, cols), 0) & (w2 - 1)) == 0)
    ranks = nn(mask(to_owner).astype(BF16), mask(before).astype(BF16))
    rank = jnp.sum(jnp.where(to_owner, ranks, 0.0), axis=0, keepdims=True).astype(I32)
    slot = step * capp + rank
    weight = weight_ref[...]
    w_hi = weight.astype(BF16).astype(F32)
    w_mid = (weight - w_hi).astype(BF16).astype(F32)
    w_lo = weight - w_hi - w_mid
    row_r = iota((16, receptors), 0)
    per_r = jnp.where(row_r == 1, hour_ref[...].astype(F32), 0.0)
    per_r = jnp.where(row_r == 3, w_hi, per_r)
    per_r = jnp.where(row_r == 4, w_mid, per_r)
    per_r = jnp.where(row_r == 5, w_lo, per_r)
    sel_r = mask(iota((receptors, cols), 0) == r_of).astype(BF16)
    values = nn(per_r.astype(BF16), sel_r)
    row_m = iota((16, cols), 0)
    values = jnp.where(row_m == 0, local_row + 1.0, values)
    values = jnp.where(row_m == 1, values + (tm * w2).astype(F32), values)
    values = jnp.where(row_m == 2, (r_of + me * receptors).astype(F32), values)
    fp = fp_ref[...]
    for w in range(w2):
        slot_w = jnp.where(w_of == w, slot, -1)
        pick = mask(iota((padded, cols), 0) == slot_w).astype(BF16)
        moved = nn(pick, fp).astype(BF16)
        for d in range(n):
            outs[d][w * capp : (w + 1) * capp, :] = moved[d * capp : (d + 1) * capp]
        if w == 0:
            meta = nt(values.astype(BF16), pick)[0:8]
            at = iota((8, padded), 1)
            for d in range(n):
                mine = jnp.where((at >= d * capp) & (at < (d + 1) * capp), meta, 0.0)
                halves = [mine[:, i : i + 256] for i in range(0, padded, 256)]
                halves += [jnp.zeros((8, 256), F32)] * (META // 8 - len(halves))
                outs[d][w2 * capp : w2 * capp + META, :] = jnp.concatenate(halves, axis=0).astype(BF16)


def pack(cfg, where, blocks, hour_start, obs_weight, placement, footprint):
    n, capp, slots, w2 = cfg["n"], cfg["capp"], cfg["slots"], cfg["w2"]
    receptors = blocks.shape[0]
    cells = footprint.shape[3]
    rows = w2 * capp + META
    vm = pl.BlockSpec(memory_space=pltpu.VMEM)
    return pl.pallas_call(
        functools.partial(pack_kernel, cfg),
        out_shape=[jax.ShapeDtypeStruct((rows, cells), BF16)] * n,
        in_specs=[pl.BlockSpec(memory_space=pltpu.SMEM)] + [vm] * 5,
        out_specs=[vm] * n,
        compiler_params=pltpu.CompilerParams(vmem_limit_bytes=VMEM_LIMIT),
        name="pack",
    )(
        where,
        blocks,
        hour_start.reshape(1, receptors),
        obs_weight.reshape(1, receptors),
        placement.reshape(1, -1),
        footprint.reshape(receptors * slots * w2, cells),
    )


def load_meta(cfg, bufs, rows):
    n, w2, capp = cfg["n"], cfg["w2"], cfg["capp"]
    total = None
    for buf, base in slots_of(bufs, rows, n):
        part = buf[base + w2 * capp : base + w2 * capp + META, :].astype(F32)
        total = part if total is None else total + part
    halves = up(n * capp, 256) // 256
    return jnp.concatenate([total[8 * i : 8 * i + 8] for i in range(halves)], axis=1)


def slots_of(bufs, rows, n):
    out = []
    for buf in bufs:
        for base in range(0, buf.shape[0], rows):
            out.append((buf, base))
    assert len(out) == n
    return out


def hour_column(meta, width):
    pick = mask(iota((8, width), 0) == 1)
    return lax.dot_general(
        meta.astype(BF16), pick.astype(BF16), (((0,), (0,)), ((), ())), preferred_element_type=F32
    )


def spread_hours(cfg, sides, metas, rows, f8_ref, base_row):
    n, w2, capp, hours, cells = cfg["n"], cfg["w2"], cfg["capp"], cfg["hours"], cfg["cells"]
    columns = [hour_column(m, cells).astype(BF16) for m in metas]
    placed = [slots_of(bufs, rows, n) for bufs in sides]
    for d in range(n):
        parts = []
        for side in range(len(sides)):
            buf, base = placed[side][d]
            first = columns[side][d * capp : (d + 1) * capp]
            for w in range(w2):
                parts.append((first + BF16(w) if w else first, buf[base + w * capp : base + (w + 1) * capp, :]))
        for h in range(hours):
            value = jnp.zeros((capp, cells), BF16)
            for first, fp in parts:
                value = jnp.where(first == BF16(h), fp, value)
            f8_ref[base_row + d * capp : base_row + (d + 1) * capp, h * cells : (h + 1) * cells] = value


def forward_kernel(cfg, nbuf, *refs):
    bufs, probes_ref, out_ref, f8_ref, meta_ref, dots_ref = (
        refs[:nbuf], refs[nbuf], refs[nbuf + 1], refs[nbuf + 2], refs[nbuf + 3], refs[nbuf + 4],
    )
    n, w2, capp, local = cfg["n"], cfg["w2"], cfg["capp"], cfg["local"]
    rows = w2 * capp + META
    used = n * capp
    k_step = probes_ref.shape[0] // local
    i = pl.program_id(0)

    @pl.when(i == 0)
    def _():
        meta = load_meta(cfg, bufs, rows)
        meta_ref[...] = meta
        spread_hours(cfg, [bufs], [meta], rows, f8_ref, 0)
        dots_ref[...] = jnp.zeros_like(dots_ref)

    own = mask(iota((local, used), 0) + 1 == meta_ref[0:1, 0:used].astype(I32))
    x = nt(probes_ref[...], f8_ref[...])
    row = iota((8, used), 0)
    acc = dots_ref[:, 0:used]
    for j in range(k_step):
        y = jnp.sum(x[j * local : (j + 1) * local] * own, axis=0, keepdims=True)
        acc = jnp.where(row == i * k_step + j, y, acc)
    dots_ref[:, 0:used] = acc

    @pl.when(i == pl.num_programs(0) - 1)
    def _():
        to_r = mask(iota((out_ref.shape[1], used), 0) == meta_ref[2:3, 0:used].astype(I32))
        out_ref[...] = lax.dot_general(
            acc, to_r, (((1,), (1,)), ((), ())), precision=lax.Precision.HIGHEST, preferred_element_type=F32
        )


def forward(cfg, bufs, probes_t):
    n, capp, hours, cells, local = cfg["n"], cfg["capp"], cfg["hours"], cfg["cells"], cfg["local"]
    used = n * capp
    vm = pl.BlockSpec(memory_space=pltpu.VMEM)
    whole = [pl.BlockSpec(b.shape, lambda i: (0, 0)) for b in bufs]
    steps = 4
    tile = probes_t.shape[0] // steps
    rp = up(n * cfg["receptors"], 128)
    return pl.pallas_call(
        functools.partial(forward_kernel, cfg, len(bufs)),
        out_shape=jax.ShapeDtypeStruct((8, rp), F32),
        grid=(steps,),
        in_specs=whole + [pl.BlockSpec((tile, hours * cells), lambda i: (i, 0))],
        out_specs=pl.BlockSpec((8, rp), lambda i: (0, 0)),
        scratch_shapes=[
            pltpu.VMEM((used, hours * cells), BF16),
            pltpu.VMEM((8, up(used, 256)), F32),
            pltpu.VMEM((8, up(used, 256)), F32),
        ],
        compiler_params=pltpu.CompilerParams(vmem_limit_bytes=VMEM_LIMIT),
        name="forward",
    )(*bufs, probes_t)


def adjoint_kernel(cfg, counts, where_ref, *refs):
    n, w2, capp, local, hours, cells = (
        cfg["n"], cfg["w2"], cfg["capp"], cfg["local"], cfg["hours"], cfg["cells"],
    )
    rows = w2 * capp + META
    used = n * capp
    kd = cfg["kd"]
    refs = list(refs)
    out_ref, f8_ref, a_ref, tiles_ref, sems = refs[-5:]
    at = 0
    for c, sides_n in enumerate(counts):
        obs = refs[at][...]
        at += 1
        sides = []
        for count in sides_n:
            sides.append(refs[at : at + count])
            at += count
        metas = [load_meta(cfg, bufs, rows) for bufs in sides]
        spread_hours(cfg, sides, metas, rows, f8_ref, c * used)
        meta = metas[0][:, 0:used]
        to_r = mask(iota((obs.shape[1], used), 0) == meta[2:3].astype(I32))
        per_entry = lax.dot_general(
            obs, to_r, (((1,), (0,)), ((), ())), precision=lax.Precision.HIGHEST, preferred_element_type=F32
        )
        per_entry = per_entry * (meta[3:4] + meta[4:5] + meta[5:6])
        own = iota((local, used), 0) + 1 == meta[0:1].astype(I32)
        row = iota((8, used), 0)
        for j in range(kd):
            term = jnp.sum(jnp.where(row == where_ref[2] * kd + j, per_entry, 0.0), axis=0, keepdims=True)
            high = term.astype(BF16).astype(F32)
            for p, part in enumerate((high, term - high)):
                a_ref[(p * kd + j) * local : (p * kd + j + 1) * local, c * used : (c + 1) * used] = jnp.where(
                    own, part, 0.0
                ).astype(BF16)
    a = a_ref[...]
    for h in range(hours):
        sums = nn(a, f8_ref[:, h * cells : (h + 1) * cells])
        for j in range(kd):
            both = sums[j * local : (j + 1) * local] + sums[(kd + j) * local : (kd + j + 1) * local]
            for t in range(cells // 128):
                tile = tiles_ref.at[j * (cells // 128) + t]
                tile[pl.ds(h, local, stride=hours), :] = both[:, t * 128 : (t + 1) * 128]
    copies = [
        pltpu.make_async_copy(tiles_ref.at[t], out_ref.at[:, pl.ds(t * 128, 128)], sems.at[t])
        for t in range(kd * cells // 128)
    ]
    for copy in copies:
        copy.start()
    for copy in copies:
        copy.wait()


def adjoint(cfg, where, columns):
    n, capp, hours, cells, local, kd = (
        cfg["n"], cfg["capp"], cfg["hours"], cfg["cells"], cfg["local"], cfg["kd"],
    )
    total = len(columns) * n * capp
    vm = pl.BlockSpec(memory_space=pltpu.VMEM)
    args, counts = [], []
    for obs, sides in columns:
        args.append(obs)
        counts.append([len(s) for s in sides])
        for s in sides:
            args += s
    return pl.pallas_call(
        functools.partial(adjoint_kernel, cfg, counts),
        out_shape=jax.ShapeDtypeStruct((local * hours, kd * cells), F32),
        in_specs=[pl.BlockSpec(memory_space=pltpu.SMEM)] + [vm] * len(args),
        out_specs=pl.BlockSpec(memory_space=pl.ANY),
        scratch_shapes=[
            pltpu.VMEM((total, hours * cells), BF16),
            pltpu.VMEM((2 * kd * local, total), BF16),
            pltpu.VMEM((kd * cells // 128, local * hours, 128), F32),
            pltpu.SemaphoreType.DMA((kd * cells // 128,)),
        ],
        compiler_params=pltpu.CompilerParams(vmem_limit_bytes=VMEM_LIMIT),
        name="adjoint",
    )(where, *args)


def shift(x, axis, d):
    n = lax.axis_size(axis)
    return lax.ppermute(x, axis, [(i, (i + d) % n) for i in range(n)])


def shards(probes, footprint, blocks, hour_start, obs_weight, placement):
    n, nreg, ntm = lax.axis_size("rcp"), lax.axis_size("reg"), lax.axis_size("tm")
    local, hours, width = probes.shape
    receptors, slots, w2, cells = footprint.shape
    k = width // cells
    cap = 3 * receptors * slots // (2 * n)
    cfg = dict(
        n=n, capp=up(cap, 16), local=local, hours=hours, cells=cells, receptors=receptors,
        slots=slots, w2=w2, kd=k // (nreg * ntm),
    )
    z, reg, tm = lax.axis_index("rcp"), lax.axis_index("reg"), lax.axis_index("tm")
    where = jnp.stack([z, tm, reg * ntm + tm]).astype(I32)
    outs = pack(cfg, where, blocks, hour_start, obs_weight, placement, footprint)
    bufs = [outs[0]] + [shift(outs[d], "rcp", d) for d in range(1, n)]
    probes_t = probes.reshape(local, hours, k, cells).transpose(2, 0, 1, 3).reshape(k * local, hours * cells)
    if n > 4:
        bufs = [jnp.concatenate(bufs, axis=0)]
    partial = forward(cfg, bufs, probes_t)
    sides = [bufs] + [[shift(b, "tm", s) for b in bufs] for s in range(1, ntm)]
    columns = [sides]
    for g in range(1, nreg):
        across = [shift(b, "reg", g) for b in bufs]
        columns.append([across] + [[shift(b, "tm", s) for b in across] for s in range(1, ntm)])
    observed = partial
    for d in range(1, n):
        observed = observed + shift(partial, "rcp", d)
    both = observed
    for s in range(1, ntm):
        both = both + shift(observed, "tm", s)
    obs = [both] + [shift(both, "reg", g) for g in range(1, nreg)]
    result = adjoint(cfg, where, list(zip(obs, columns)))
    return result.reshape(local, hours, cfg["kd"] * cells)


def solution(mesh):
    return jax.shard_map(
        shards,
        mesh=mesh,
        in_specs=(
            P(("inv", "rcp"), None, None),
            P(("inv", "rcp", "reg"), None, "tm", None),
            P(("inv", "rcp", "reg"), None),
            P(("inv", "rcp", "reg")),
            P(("inv", "rcp", "reg")),
            P("inv"),
        ),
        out_specs=P(("inv", "rcp"), None, ("reg", "tm")),
        check_vma=False,
    )
```

```python
import functools

import jax
import jax.numpy as jnp
from jax import lax
from jax.experimental import pallas as pl
from jax.experimental.pallas import tpu as pltpu
from jax.sharding import PartitionSpec as P

F32 = jnp.float32
BF16 = jnp.bfloat16
I32 = jnp.int32
META = 16
VMEM_LIMIT = 48 * 1024 * 1024


def up(x, m):
    return (x + m - 1) // m * m


def log2(x):
    assert x & (x - 1) == 0
    return x.bit_length() - 1


def iota(shape, axis):
    return lax.broadcasted_iota(I32, shape, axis)


def mask(cond):
    return jnp.where(cond, jnp.float32(1), jnp.float32(0))


def nt(a, b):
    return lax.dot_general(a, b, (((1,), (1,)), ((), ())), preferred_element_type=F32)


def nn(a, b):
    return lax.dot_general(a, b, (((1,), (0,)), ((), ())), preferred_element_type=F32)


def pack_kernel(cfg, where_ref, blocks_hbm, hour_hbm, weight_hbm, place_hbm, fp_ref, *refs):
    n, capp, local_blocks, slots, w2 = cfg["n"], cfg["capp"], cfg["local"], cfg["slots"], cfg["w2"]
    outs, (blocks_ref, hour_ref, weight_ref, place_ref, sems) = refs[:n], refs[n:]
    pairs = ((blocks_hbm, blocks_ref), (place_hbm, place_ref), (hour_hbm, hour_ref), (weight_hbm, weight_ref))
    copies = [pltpu.make_async_copy(src, dst, sems.at[i]) for i, (src, dst) in enumerate(pairs)]
    for copy in copies:
        copy.start()
    receptors = blocks_ref.shape[0]
    cols = receptors * slots * w2
    ids = place_ref.shape[1]
    used = n * capp
    padded = up(used, 256)
    half = n // 2
    me = where_ref[0]
    tm = where_ref[1]
    lane = iota((1, cols), 1)
    entry = lane >> log2(w2)
    w_of = lane & (w2 - 1)
    s_of = entry & (slots - 1)
    r_of = entry >> log2(slots)
    sel_s = mask(iota((slots, cols), 0) == s_of).astype(BF16)
    sel_r = mask(iota((receptors, cols), 0) == r_of).astype(BF16)
    before = ((iota((cols, cols), 0) >> log2(w2)) < entry) & ((iota((cols, cols), 0) & (w2 - 1)) == 0)
    before = mask(before).astype(BF16)
    for copy in copies:
        copy.wait()
    b = blocks_ref[...]
    high = (b >> 6).astype(F32).astype(BF16)
    low = (b & 63).astype(F32).astype(BF16)
    spread = nn(high, sel_s) * 64.0 + nn(low, sel_s)
    on_row = iota((receptors, cols), 0) == r_of
    geo = jnp.sum(jnp.where(on_row, spread, 0.0), axis=0, keepdims=True).astype(I32)
    place = place_ref[...]
    row16 = iota((16, ids), 0)
    owner_tab = (place >> log2(local_blocks)).astype(F32)
    local_tab = (place & (local_blocks - 1)).astype(F32)
    tab = jnp.where(row16 == 0, owner_tab, jnp.where(row16 == 1, local_tab, 0.0)).astype(BF16)
    found = nn(tab, mask(iota((ids, cols), 0) == geo).astype(BF16))
    step = found[0:1].astype(I32) - me
    step = jnp.where(step < 0, step + n, step)
    local_row = found[1:2]
    to_owner = iota((up(n, 16), cols), 0) == step
    ranks = nn(mask(to_owner).astype(BF16), before)
    rank = jnp.sum(jnp.where(to_owner, ranks, 0.0), axis=0, keepdims=True).astype(I32)
    slot = step * capp + rank
    weight = weight_ref[...]
    w_hi = weight.astype(BF16).astype(F32)
    w_mid = (weight - w_hi).astype(BF16).astype(F32)
    w_lo = weight - w_hi - w_mid
    row_r = iota((16, receptors), 0)
    per_r = jnp.where(row_r == 1, hour_ref[...].astype(F32), 0.0)
    per_r = jnp.where(row_r == 3, w_hi, per_r)
    per_r = jnp.where(row_r == 4, w_mid, per_r)
    per_r = jnp.where(row_r == 5, w_lo, per_r)
    values = nn(per_r.astype(BF16), sel_r)
    row_m = iota((16, cols), 0)
    values = jnp.where(row_m == 0, local_row + 1.0, values)
    values = jnp.where(row_m == 1, values + (tm * w2).astype(F32), values)
    values = jnp.where(row_m == 2, (r_of + me * receptors).astype(F32), values)
    fp = fp_ref[...]
    for w in range(w2):
        slot_w = jnp.where(w_of == w, slot, -1)
        pick = mask(iota((padded, cols), 0) == slot_w).astype(BF16)
        moved = nn(pick, fp).astype(BF16)
        for d in range(n):
            outs[d][w * capp : (w + 1) * capp, :] = moved[d * capp : (d + 1) * capp]
        if w == 0:
            meta = nt(values.astype(BF16), pick)
            at = iota((16, half * capp), 1)
            for d in range(n):
                base = d // half * half * capp
                place_d = d % half * capp
                mine = meta[:, base : base + half * capp]
                mine = jnp.where((at >= place_d) & (at < place_d + capp), mine, 0.0).astype(BF16)
                outs[d][w2 * capp : w2 * capp + META, :] = jnp.zeros((META, outs[d].shape[1]), BF16)
                outs[d][w2 * capp : w2 * capp + META, 0 : half * capp] = mine


def pack(cfg, where, blocks, hour_start, obs_weight, placement, footprint):
    n, capp, slots, w2 = cfg["n"], cfg["capp"], cfg["slots"], cfg["w2"]
    receptors = blocks.shape[0]
    cells = footprint.shape[3]
    rows = w2 * capp + META
    hour_start, obs_weight, placement = (
        hour_start.reshape(1, receptors), obs_weight.reshape(1, receptors), placement.reshape(1, -1),
    )
    vm = pl.BlockSpec(memory_space=pltpu.VMEM)
    return pl.pallas_call(
        functools.partial(pack_kernel, cfg),
        out_shape=[jax.ShapeDtypeStruct((rows, cells), BF16)] * n,
        in_specs=[pl.BlockSpec(memory_space=pltpu.SMEM)] + [pl.BlockSpec(memory_space=pltpu.HBM)] * 4 + [vm],
        out_specs=[vm] * n,
        scratch_shapes=[
            pltpu.VMEM(blocks.shape, I32),
            pltpu.VMEM(hour_start.shape, I32),
            pltpu.VMEM(obs_weight.shape, F32),
            pltpu.VMEM(placement.shape, I32),
            pltpu.SemaphoreType.DMA((4,)),
        ],
        compiler_params=pltpu.CompilerParams(vmem_limit_bytes=VMEM_LIMIT),
        name="pack",
    )(where, blocks, hour_start, obs_weight, placement, footprint.reshape(receptors * slots * w2, cells))


def slots_of(bufs, rows):
    return [(buf, base) for buf in bufs for base in range(0, buf.shape[0], rows)]


def load_meta(cfg, placed):
    w2, capp = cfg["w2"], cfg["capp"]
    total = None
    for buf, base in placed:
        part = buf[base + w2 * capp : base + w2 * capp + META, :].astype(F32)
        total = part if total is None else total + part
    return total[:, 0 : len(placed) * capp]


def hour_column(meta, width):
    pick = mask(iota((16, width), 0) == 1)
    return lax.dot_general(
        meta.astype(BF16), pick.astype(BF16), (((0,), (0,)), ((), ())), preferred_element_type=F32
    )


def spread_hours(cfg, sides, metas, f8_ref, base_row):
    w2, capp, hours, cells = cfg["w2"], cfg["capp"], cfg["hours"], cfg["cells"]
    columns = [hour_column(m, cells).astype(BF16) for m in metas]
    for d in range(len(sides[0])):
        parts = []
        for side in range(len(sides)):
            buf, base = sides[side][d]
            first = columns[side][d * capp : (d + 1) * capp]
            for w in range(w2):
                parts.append((first + BF16(w) if w else first, buf[base + w * capp : base + (w + 1) * capp, :]))
        for h in range(hours):
            value = jnp.zeros((capp, cells), BF16)
            for first, fp in parts:
                value = jnp.where(first == BF16(h), fp, value)
            f8_ref[base_row + d * capp : base_row + (d + 1) * capp, h * cells : (h + 1) * cells] = value


def forward_kernel(cfg, nbuf, *refs):
    bufs, (probes_ref, sofar_ref, out_ref, f8_ref) = refs[:nbuf], refs[nbuf:]
    local, k = cfg["local"], cfg["k"]
    placed = slots_of(bufs, cfg["rows"])
    meta = load_meta(cfg, placed)
    used = meta.shape[1]
    spread_hours(cfg, [placed], [meta], f8_ref, 0)
    own = iota((local, used), 0) + 1 == meta[0:1].astype(I32)
    row = iota((8, used), 0)
    dots = jnp.zeros((8, used), F32)
    f8 = f8_ref[...]
    for j in range(k):
        x = nt(probes_ref[j * local : (j + 1) * local, :], f8)
        y = jnp.sum(jnp.where(own, x, 0.0), axis=0, keepdims=True)
        dots = jnp.where(row == j, y, dots)
    to_r = mask(iota((out_ref.shape[1], used), 0) == meta[2:3].astype(I32))
    out_ref[...] = sofar_ref[...] + lax.dot_general(
        dots, to_r, (((1,), (1,)), ((), ())), precision=lax.Precision.HIGHEST, preferred_element_type=F32
    )


def forward(cfg, bufs, probes_t, sofar, name):
    n, capp, hours, cells = cfg["n"], cfg["capp"], cfg["hours"], cfg["cells"]
    used = n // 2 * capp
    vm = pl.BlockSpec(memory_space=pltpu.VMEM)
    return pl.pallas_call(
        functools.partial(forward_kernel, cfg, len(bufs)),
        out_shape=jax.ShapeDtypeStruct(sofar.shape, F32),
        in_specs=[vm] * (len(bufs) + 2),
        out_specs=vm,
        scratch_shapes=[pltpu.VMEM((used, hours * cells), BF16)],
        compiler_params=pltpu.CompilerParams(vmem_limit_bytes=VMEM_LIMIT),
        cost_estimate=pl.CostEstimate(
            flops=2 * used * probes_t.size, bytes_accessed=2 * probes_t.size, transcendentals=0
        ),
        name=name,
    )(*bufs, probes_t, sofar)


def prepare_kernel(cfg, counts, *refs):
    n, capp = cfg["n"], cfg["capp"]
    f8_ref, meta_ref, zero_ref = refs[-3:]
    zero_ref[...] = jnp.zeros_like(zero_ref)
    at = 0
    for c, halves in enumerate(counts):
        metas = []
        for i, sides_n in enumerate(halves):
            sides = []
            for count in sides_n:
                sides.append(slots_of(refs[at : at + count], cfg["rows"]))
                at += count
            side_metas = [load_meta(cfg, placed) for placed in sides]
            spread_hours(cfg, sides, side_metas, f8_ref, (2 * c + i) * (n // 2) * capp)
            metas.append(side_metas[0][0:8])
        meta_ref[:, c * n * capp : (c + 1) * n * capp] = jnp.concatenate(metas, axis=1)


def prepare(cfg, columns, zero_shape):
    n, capp, hours, cells = cfg["n"], cfg["capp"], cfg["hours"], cfg["cells"]
    total = len(columns) * n * capp
    args = [b for halves in columns for sides in halves for side in sides for b in side]
    counts = [[[len(side) for side in sides] for sides in halves] for halves in columns]
    vm = pl.BlockSpec(memory_space=pltpu.VMEM)
    return pl.pallas_call(
        functools.partial(prepare_kernel, cfg, counts),
        out_shape=[
            jax.ShapeDtypeStruct((total, hours * cells), BF16),
            jax.ShapeDtypeStruct((8, total), F32),
            jax.ShapeDtypeStruct(zero_shape, F32),
        ],
        in_specs=[vm] * len(args),
        out_specs=[vm] * 3,
        compiler_params=pltpu.CompilerParams(vmem_limit_bytes=VMEM_LIMIT),
        cost_estimate=pl.CostEstimate(flops=0, bytes_accessed=6 * total * hours * cells, transcendentals=0),
        name="prepare",
    )(*args)


def adjoint_kernel(cfg, parts, where_ref, meta_ref, f8_ref, *refs):
    n, capp, local, hours, cells, kd = (
        cfg["n"], cfg["capp"], cfg["local"], cfg["hours"], cfg["cells"], cfg["kd"],
    )
    obs_refs, (out_ref, a_ref, tiles_ref, sems) = refs[:-4], refs[-4:]
    used = n * capp
    per_k = cells // 128
    for c in range(len(obs_refs) // parts):
        obs = obs_refs[c * parts][...]
        for i in range(1, parts):
            obs = obs + obs_refs[c * parts + i][...]
        meta = meta_ref[:, c * used : (c + 1) * used]
        to_r = mask(iota((obs.shape[1], used), 0) == meta[2:3].astype(I32))
        per_entry = lax.dot_general(
            obs, to_r, (((1,), (0,)), ((), ())), precision=lax.Precision.HIGHEST, preferred_element_type=F32
        )
        per_entry = per_entry * (meta[3:4] + meta[4:5] + meta[5:6])
        own = iota((local, used), 0) + 1 == meta[0:1].astype(I32)
        row = iota((8, used), 0)
        for j in range(kd):
            term = jnp.sum(jnp.where(row == where_ref[2] * kd + j, per_entry, 0.0), axis=0, keepdims=True)
            high = term.astype(BF16).astype(F32)
            for p, part in enumerate((high, term - high)):
                a_ref[(2 * j + p) * local : (2 * j + p + 1) * local, c * used : (c + 1) * used] = jnp.where(
                    own, part, 0.0
                ).astype(BF16)
    copies = []
    for j in range(kd):
        a = a_ref[2 * j * local : 2 * (j + 1) * local, :]
        for h in range(hours):
            sums = nn(a, f8_ref[:, h * cells : (h + 1) * cells])
            both = sums[0:local] + sums[local : 2 * local]
            for t in range(per_k):
                tiles_ref.at[j * per_k + t][pl.ds(h, local, stride=hours), :] = both[:, t * 128 : (t + 1) * 128]
        for t in range(j * per_k, (j + 1) * per_k):
            copy = pltpu.make_async_copy(tiles_ref.at[t], out_ref.at[:, pl.ds(t * 128, 128)], sems.at[t])
            copy.start()
            copies.append(copy)
    for copy in copies:
        copy.wait()


def adjoint(cfg, where, f8, meta, observed):
    hours, cells, local, kd = cfg["hours"], cfg["cells"], cfg["local"], cfg["kd"]
    total = f8.shape[0]
    parts = len(observed[0])
    args = [o for column in observed for o in column]
    vm = pl.BlockSpec(memory_space=pltpu.VMEM)
    return pl.pallas_call(
        functools.partial(adjoint_kernel, cfg, parts),
        out_shape=jax.ShapeDtypeStruct((local * hours, kd * cells), F32),
        in_specs=[pl.BlockSpec(memory_space=pltpu.SMEM)] + [vm] * (2 + len(args)),
        out_specs=pl.BlockSpec(memory_space=pl.ANY),
        scratch_shapes=[
            pltpu.VMEM((2 * kd * local, total), BF16),
            pltpu.VMEM((kd * cells // 128, local * hours, 128), F32),
            pltpu.SemaphoreType.DMA((kd * cells // 128,)),
        ],
        compiler_params=pltpu.CompilerParams(vmem_limit_bytes=VMEM_LIMIT),
        name="adjoint",
    )(where, meta, f8, *args)


def shift(x, axis, d):
    n = lax.axis_size(axis)
    return lax.ppermute(x, axis, [(i, (i + d) % n) for i in range(n)])


def shift2(x, g, s):
    nreg, ntm = lax.axis_size("reg"), lax.axis_size("tm")
    pairs = [
        (r * ntm + t, (r + g) % nreg * ntm + (t + s) % ntm) for r in range(nreg) for t in range(ntm)
    ]
    return lax.ppermute(x, ("reg", "tm"), pairs)


def shards(probes, footprint, blocks, hour_start, obs_weight, placement):
    n, nreg, ntm = lax.axis_size("rcp"), lax.axis_size("reg"), lax.axis_size("tm")
    local, hours, width = probes.shape
    receptors, slots, w2, cells = footprint.shape
    k = width // cells
    capp = up(3 * receptors * slots // (2 * n), 16)
    cfg = dict(
        n=n, capp=capp, local=local, hours=hours, cells=cells, slots=slots, w2=w2, k=k,
        kd=k // (nreg * ntm), rows=w2 * capp + META,
    )
    z, reg, tm = lax.axis_index("rcp"), lax.axis_index("reg"), lax.axis_index("tm")
    where = jnp.stack([z, tm, reg * ntm + tm]).astype(I32)
    outs = pack(cfg, where, blocks, hour_start, obs_weight, placement, footprint)
    bufs = [outs[0]] + [shift(outs[d], "rcp", d) for d in range(1, n)]
    probes_t = probes.reshape(local, hours, k, cells).transpose(2, 0, 1, 3).reshape(k * local, hours * cells)
    halves = [bufs[: n // 2], bufs[n // 2 :]]
    if n > 4:
        halves = [[jnp.concatenate(half, axis=0)] for half in halves]
    partial = jnp.zeros((8, up(n * receptors, 128)), F32)
    for i, half in enumerate(halves):
        partial = forward(cfg, half, probes_t, partial, f"forward{i}")
    columns = [[[half] + [[shift(b, "tm", s) for b in half] for s in range(1, ntm)] for half in halves]]
    for g in range(1, nreg):
        across = [[shift(b, "reg", g) for b in half] for half in halves]
        columns.append([[half] + [[shift(b, "tm", s) for b in half] for s in range(1, ntm)] for half in across])
    f8, meta, zero = prepare(cfg, columns, partial.shape)
    observed = partial + zero
    for d in range(1, n):
        observed = observed + shift(partial, "rcp", d)
    observed = [[shift2(observed, g, s) if g or s else observed for s in range(ntm)] for g in range(nreg)]
    result = adjoint(cfg, where, f8, meta, observed)
    return result.reshape(local, hours, cfg["kd"] * cells)


def solution(mesh):
    return jax.shard_map(
        shards,
        mesh=mesh,
        in_specs=(
            P(("inv", "rcp"), None, None),
            P(("inv", "rcp", "reg"), None, "tm", None),
            P(("inv", "rcp", "reg"), None),
            P(("inv", "rcp", "reg")),
            P(("inv", "rcp", "reg")),
            P("inv"),
        ),
        out_specs=P(("inv", "rcp"), None, ("reg", "tm")),
        check_vma=False,
    )
```

```python
import functools

import jax
import jax.numpy as jnp
from jax import lax
from jax.experimental import pallas as pl
from jax.experimental.pallas import tpu as pltpu
from jax.sharding import PartitionSpec as P

F32 = jnp.float32
BF16 = jnp.bfloat16
I32 = jnp.int32
META = 16
VMEM_LIMIT = 48 * 1024 * 1024
FORWARD_BYTES = 0


def up(x, m):
    return (x + m - 1) // m * m


def log2(x):
    assert x & (x - 1) == 0
    return x.bit_length() - 1


def iota(shape, axis):
    return lax.broadcasted_iota(I32, shape, axis)


def mask(cond):
    return jnp.where(cond, jnp.float32(1), jnp.float32(0))


def nt(a, b):
    return lax.dot_general(a, b, (((1,), (1,)), ((), ())), preferred_element_type=F32)


def nn(a, b):
    return lax.dot_general(a, b, (((1,), (0,)), ((), ())), preferred_element_type=F32)


def pack_kernel(cfg, where_ref, small_ref, fp_ref, *outs):
    n, capp, local_blocks, slots, w2 = cfg["n"], cfg["capp"], cfg["local"], cfg["slots"], cfg["w2"]
    receptors = cfg["receptors"]
    cols = receptors * slots * w2
    ids = small_ref.shape[1]
    at_place = receptors
    used = n * capp
    padded = up(used, 256)
    half = n // 2
    me = where_ref[0]
    tm = where_ref[1]
    lane = iota((1, cols), 1)
    entry = lane >> log2(w2)
    w_of = lane & (w2 - 1)
    s_of = entry & (slots - 1)
    r_of = entry >> log2(slots)
    sel_s = mask(iota((slots, cols), 0) == s_of).astype(BF16)
    sel_r = mask(iota((receptors, cols), 0) == r_of).astype(BF16)
    before = ((iota((cols, cols), 0) >> log2(w2)) < entry) & ((iota((cols, cols), 0) & (w2 - 1)) == 0)
    before = mask(before).astype(BF16)
    b = small_ref[0:receptors, 0:slots].astype(I32)
    high = (b >> 6).astype(F32).astype(BF16)
    low = (b & 63).astype(F32).astype(BF16)
    spread = nn(high, sel_s) * 64.0 + nn(low, sel_s)
    on_row = iota((receptors, cols), 0) == r_of
    geo = jnp.sum(jnp.where(on_row, spread, 0.0), axis=0, keepdims=True).astype(I32)
    place = small_ref[at_place : at_place + 1, :].astype(I32)
    row16 = iota((16, ids), 0)
    owner_tab = (place >> log2(local_blocks)).astype(F32)
    local_tab = (place & (local_blocks - 1)).astype(F32)
    tab = jnp.where(row16 == 0, owner_tab, jnp.where(row16 == 1, local_tab, 0.0)).astype(BF16)
    found = nn(tab, mask(iota((ids, cols), 0) == geo).astype(BF16))
    step = found[0:1].astype(I32) - me
    step = jnp.where(step < 0, step + n, step)
    local_row = found[1:2]
    to_owner = iota((up(n, 16), cols), 0) == step
    ranks = nn(mask(to_owner).astype(BF16), before)
    rank = jnp.sum(jnp.where(to_owner, ranks, 0.0), axis=0, keepdims=True).astype(I32)
    slot = step * capp + rank
    hour = small_ref[at_place + 1 : at_place + 2, 0:receptors]
    weight = small_ref[at_place + 2 : at_place + 3, 0:receptors]
    w_hi = weight.astype(BF16).astype(F32)
    w_mid = (weight - w_hi).astype(BF16).astype(F32)
    w_lo = weight - w_hi - w_mid
    row_r = iota((16, receptors), 0)
    per_r = jnp.where(row_r == 1, hour, 0.0)
    per_r = jnp.where(row_r == 3, w_hi, per_r)
    per_r = jnp.where(row_r == 4, w_mid, per_r)
    per_r = jnp.where(row_r == 5, w_lo, per_r)
    values = nn(per_r.astype(BF16), sel_r)
    row_m = iota((16, cols), 0)
    values = jnp.where(row_m == 0, local_row + 1.0, values)
    values = jnp.where(row_m == 1, values + (tm * w2).astype(F32), values)
    values = jnp.where(row_m == 2, (r_of + me * receptors).astype(F32), values)
    fp = fp_ref[...]
    for w in range(w2):
        slot_w = jnp.where(w_of == w, slot, -1)
        pick = mask(iota((padded, cols), 0) == slot_w).astype(BF16)
        moved = nn(pick, fp).astype(BF16)
        for d in range(n):
            outs[d][w * capp : (w + 1) * capp, :] = moved[d * capp : (d + 1) * capp]
        if w == 0:
            meta = nt(values.astype(BF16), pick)
            at = iota((16, half * capp), 1)
            for d in range(n):
                base = d // half * half * capp
                place_d = d % half * capp
                mine = meta[:, base : base + half * capp]
                mine = jnp.where((at >= place_d) & (at < place_d + capp), mine, 0.0).astype(BF16)
                outs[d][w2 * capp : w2 * capp + META, :] = jnp.zeros((META, outs[d].shape[1]), BF16)
                outs[d][w2 * capp : w2 * capp + META, 0 : half * capp] = mine


def pack(cfg, where, blocks, hour_start, obs_weight, placement, footprint):
    n, capp, slots, w2 = cfg["n"], cfg["capp"], cfg["slots"], cfg["w2"]
    receptors = blocks.shape[0]
    cells = footprint.shape[3]
    rows = w2 * capp + META
    ids = placement.shape[0]
    height = up(receptors + 3, 8)

    def put(x, at):
        x = x.astype(F32)
        return jnp.pad(x, ((at, height - at - x.shape[0]), (0, ids - x.shape[1])))

    small = put(blocks, 0) + put(placement[None], receptors)
    small = small + put(hour_start[None], receptors + 1) + put(obs_weight[None], receptors + 2)
    vm = pl.BlockSpec(memory_space=pltpu.VMEM)
    return pl.pallas_call(
        functools.partial(pack_kernel, cfg),
        out_shape=[jax.ShapeDtypeStruct((rows, cells), BF16)] * n,
        in_specs=[pl.BlockSpec(memory_space=pltpu.SMEM), vm, vm],
        out_specs=[vm] * n,
        compiler_params=pltpu.CompilerParams(vmem_limit_bytes=VMEM_LIMIT),
        name="pack",
    )(where, small, footprint.reshape(receptors * slots * w2, cells))


def slots_of(bufs, rows):
    return [(buf, base) for buf in bufs for base in range(0, buf.shape[0], rows)]


def load_meta(cfg, placed):
    w2, capp = cfg["w2"], cfg["capp"]
    total = None
    for buf, base in placed:
        part = buf[base + w2 * capp : base + w2 * capp + META, :].astype(F32)
        total = part if total is None else total + part
    return total[:, 0 : len(placed) * capp]


def hour_column(meta, width):
    pick = mask(iota((16, width), 0) == 1)
    return lax.dot_general(
        meta.astype(BF16), pick.astype(BF16), (((0,), (0,)), ((), ())), preferred_element_type=F32
    )


def spread_hours(cfg, sides, metas, f8_ref, base_row):
    w2, capp, hours, cells = cfg["w2"], cfg["capp"], cfg["hours"], cfg["cells"]
    columns = [hour_column(m, cells).astype(BF16) for m in metas]
    for d in range(len(sides[0])):
        parts = []
        for side in range(len(sides)):
            buf, base = sides[side][d]
            first = columns[side][d * capp : (d + 1) * capp]
            for w in range(w2):
                parts.append((first + BF16(w) if w else first, buf[base + w * capp : base + (w + 1) * capp, :]))
        for h in range(hours):
            value = jnp.zeros((capp, cells), BF16)
            for first, fp in parts:
                value = jnp.where(first == BF16(h), fp, value)
            f8_ref[base_row + d * capp : base_row + (d + 1) * capp, h * cells : (h + 1) * cells] = value


def after_kernel(x_ref, unread_ref, out_ref):
    out_ref[...] = x_ref[...]


def after(x, first):
    return pl.pallas_call(
        after_kernel,
        out_shape=jax.ShapeDtypeStruct(x.shape, x.dtype),
        grid=(1,),
        in_specs=[pl.BlockSpec(x.shape, lambda i: (0, 0)), pl.BlockSpec((16, 128), lambda i: (0, 0))],
        out_specs=pl.BlockSpec(x.shape, lambda i: (0, 0)),
        compiler_params=pltpu.CompilerParams(vmem_limit_bytes=4 * 1024 * 1024),
        cost_estimate=pl.CostEstimate(flops=0, bytes_accessed=2 * x.size, transcendentals=0),
        name="after",
    )(x, first)


def forward_kernel(cfg, counts, *refs):
    local, k, rows, capp = cfg["local"], cfg["k_core"], cfg["rows"], cfg["capp"]
    half = cfg["n"] // 2 * capp
    probes_ref, out_ref, f8_ref = refs[-3:]
    at = 0
    firsts = []
    for i, sides_n in enumerate(counts):
        sides = []
        for count in sides_n:
            sides.append(slots_of(refs[at : at + count], rows))
            at += count
        metas = [load_meta(cfg, placed) for placed in sides]
        spread_hours(cfg, sides, metas, f8_ref, i * half)
        firsts.append(metas[0][0:8])
    meta = jnp.concatenate(firsts, axis=1)
    used = meta.shape[1]
    own = iota((local, used), 0) + 1 == meta[0:1].astype(I32)
    row = iota((8, used), 0)
    dots = jnp.zeros((8, used), F32)
    f8 = f8_ref[...]
    for j in range(k):
        x = nt(probes_ref[j * local : (j + 1) * local, :], f8)
        y = jnp.sum(jnp.where(own, x, 0.0), axis=0, keepdims=True)
        dots = jnp.where(row == j, y, dots)
    to_r = mask(iota((out_ref.shape[1], used), 0) == meta[2:3].astype(I32))
    out_ref[...] = lax.dot_general(
        dots, to_r, (((1,), (1,)), ((), ())), precision=lax.Precision.HIGHEST, preferred_element_type=F32
    )


def forward(cfg, own, probes_t, out_shape):
    n, capp, hours, cells = cfg["n"], cfg["capp"], cfg["hours"], cfg["cells"]
    args = [b for half in own for side in half for b in side]
    counts = [[len(side) for side in half] for half in own]
    vm = pl.BlockSpec(memory_space=pltpu.VMEM)
    return pl.pallas_call(
        functools.partial(forward_kernel, cfg, counts),
        out_shape=jax.ShapeDtypeStruct(out_shape, F32),
        in_specs=[vm] * (len(args) + 1),
        out_specs=vm,
        scratch_shapes=[pltpu.VMEM((n * capp, hours * cells), BF16)],
        compiler_params=pltpu.CompilerParams(vmem_limit_bytes=VMEM_LIMIT),
        cost_estimate=pl.CostEstimate(flops=0, bytes_accessed=FORWARD_BYTES, transcendentals=0),
        name="forward",
    )(*args, probes_t)


def prepare_kernel(cfg, counts, *refs):
    n, capp = cfg["n"], cfg["capp"]
    f8_ref, meta_ref, zero_ref = refs[-3:]
    zero_ref[...] = jnp.zeros_like(zero_ref)
    at = 0
    for c, halves in enumerate(counts):
        metas = []
        for i, sides_n in enumerate(halves):
            sides = []
            for count in sides_n:
                sides.append(slots_of(refs[at : at + count], cfg["rows"]))
                at += count
            side_metas = [load_meta(cfg, placed) for placed in sides]
            spread_hours(cfg, sides, side_metas, f8_ref, (2 * c + i) * (n // 2) * capp)
            metas.append(side_metas[0][0:8])
        meta_ref[:, c * n * capp : (c + 1) * n * capp] = jnp.concatenate(metas, axis=1)


def prepare(cfg, columns, zero_shape):
    n, capp, hours, cells = cfg["n"], cfg["capp"], cfg["hours"], cfg["cells"]
    total = len(columns) * n * capp
    args = [b for halves in columns for sides in halves for side in sides for b in side]
    counts = [[[len(side) for side in sides] for sides in halves] for halves in columns]
    vm = pl.BlockSpec(memory_space=pltpu.VMEM)
    return pl.pallas_call(
        functools.partial(prepare_kernel, cfg, counts),
        out_shape=[
            jax.ShapeDtypeStruct((total, hours * cells), BF16),
            jax.ShapeDtypeStruct((8, total), F32),
            jax.ShapeDtypeStruct(zero_shape, F32),
        ],
        in_specs=[vm] * len(args),
        out_specs=[vm] * 3,
        compiler_params=pltpu.CompilerParams(vmem_limit_bytes=VMEM_LIMIT),
        cost_estimate=pl.CostEstimate(flops=0, bytes_accessed=6 * total * hours * cells, transcendentals=0),
        name="prepare",
    )(*args)


def adjoint_kernel(cfg, parts, where_ref, meta_ref, f8_ref, *refs):
    n, capp, local, hours, cells, kd = (
        cfg["n"], cfg["capp"], cfg["local"], cfg["hours"], cfg["cells"], cfg["kd"],
    )
    obs_refs, (out_ref, a_ref, tiles_ref, sems) = refs[:-4], refs[-4:]
    used = n * capp
    per_k = cells // 128
    for c in range(len(obs_refs) // parts):
        obs = obs_refs[c * parts][...]
        for i in range(1, parts):
            obs = obs + obs_refs[c * parts + i][...]
        meta = meta_ref[:, c * used : (c + 1) * used]
        to_r = mask(iota((obs.shape[1], used), 0) == meta[2:3].astype(I32))
        per_entry = lax.dot_general(
            obs, to_r, (((1,), (0,)), ((), ())), precision=lax.Precision.HIGHEST, preferred_element_type=F32
        )
        per_entry = per_entry * (meta[3:4] + meta[4:5] + meta[5:6])
        own = iota((local, used), 0) + 1 == meta[0:1].astype(I32)
        row = iota((8, used), 0)
        for j in range(kd):
            term = jnp.sum(jnp.where(row == where_ref[2] * kd + j, per_entry, 0.0), axis=0, keepdims=True)
            high = term.astype(BF16).astype(F32)
            for p, part in enumerate((high, term - high)):
                a_ref[(2 * j + p) * local : (2 * j + p + 1) * local, c * used : (c + 1) * used] = jnp.where(
                    own, part, 0.0
                ).astype(BF16)
    copies = []
    for j in range(kd):
        a = a_ref[2 * j * local : 2 * (j + 1) * local, :]
        for h in range(hours):
            sums = nn(a, f8_ref[:, h * cells : (h + 1) * cells])
            both = sums[0:local] + sums[local : 2 * local]
            for t in range(per_k):
                tiles_ref.at[j * per_k + t][pl.ds(h, local, stride=hours), :] = both[:, t * 128 : (t + 1) * 128]
        for t in range(j * per_k, (j + 1) * per_k):
            copy = pltpu.make_async_copy(tiles_ref.at[t], out_ref.at[:, pl.ds(t * 128, 128)], sems.at[t])
            copy.start()
            copies.append(copy)
    for copy in copies:
        copy.wait()


def adjoint(cfg, where, f8, meta, observed):
    hours, cells, local, kd = cfg["hours"], cfg["cells"], cfg["local"], cfg["kd"]
    total = f8.shape[0]
    parts = len(observed[0])
    args = [o for column in observed for o in column]
    vm = pl.BlockSpec(memory_space=pltpu.VMEM)
    return pl.pallas_call(
        functools.partial(adjoint_kernel, cfg, parts),
        out_shape=jax.ShapeDtypeStruct((local * hours, kd * cells), F32),
        in_specs=[pl.BlockSpec(memory_space=pltpu.SMEM)] + [vm] * (2 + len(args)),
        out_specs=pl.BlockSpec(memory_space=pl.ANY),
        scratch_shapes=[
            pltpu.VMEM((2 * kd * local, total), BF16),
            pltpu.VMEM((kd * cells // 128, local * hours, 128), F32),
            pltpu.SemaphoreType.DMA((kd * cells // 128,)),
        ],
        compiler_params=pltpu.CompilerParams(vmem_limit_bytes=VMEM_LIMIT),
        name="adjoint",
    )(where, meta, f8, *args)


def shift(x, axis, d):
    n = lax.axis_size(axis)
    return lax.ppermute(x, axis, [(i, (i + d) % n) for i in range(n)])


def shards(probes, footprint, blocks, hour_start, obs_weight, placement):
    n, nreg, ntm = lax.axis_size("rcp"), lax.axis_size("reg"), lax.axis_size("tm")
    local, hours, width = probes.shape
    receptors, slots, w2, cells = footprint.shape
    k = width // cells
    kd = k // (nreg * ntm)
    capp = up(3 * receptors * slots // (2 * n), 16)
    cfg = dict(
        n=n, capp=capp, local=local, hours=hours, cells=cells, receptors=receptors, slots=slots, w2=w2,
        kd=kd, k_core=nreg * kd, rows=w2 * capp + META,
    )
    z, reg, tm = lax.axis_index("rcp"), lax.axis_index("reg"), lax.axis_index("tm")
    where = jnp.stack([z, tm, reg]).astype(I32)
    outs = pack(cfg, where, blocks, hour_start, obs_weight, placement, footprint)
    probes_t = lax.dynamic_index_in_dim(probes.reshape(local, hours, nreg, ntm, kd, cells), tm, 3, keepdims=False)
    probes_t = probes_t.transpose(2, 3, 0, 1, 4).reshape(nreg * kd * local, hours * cells)

    def with_cores(half):
        return [half] + [[shift(b, "tm", s) for b in half] for s in range(1, ntm)]

    mine = after(outs[0], probes_t)
    bufs = [mine] + [shift(outs[d], "rcp", d) for d in range(1, n)]
    halves = [bufs[: n // 2], bufs[n // 2 :]]
    if n > 4:
        halves = [[jnp.concatenate(half, axis=0)] for half in halves]
    own = [with_cores(half) for half in halves]
    partial = forward(cfg, own, probes_t, (8, up(n * receptors, 128)))
    columns = [own]
    for g in range(1, nreg):
        across = [[shift(b, "reg", g) for b in half] for half in halves]
        columns.append([with_cores(half) for half in across])
    f8, meta, zero = prepare(cfg, columns, partial.shape)
    observed = partial + zero
    for d in range(1, n):
        observed = observed + shift(partial, "rcp", d)
    observed = [[shift(observed, "reg", g) if g else observed] for g in range(nreg)]
    result = adjoint(cfg, where, f8, meta, observed)
    return result.reshape(local, hours, kd * cells)


def solution(mesh):
    return jax.shard_map(
        shards,
        mesh=mesh,
        in_specs=(
            P(("inv", "rcp"), None, None),
            P(("inv", "rcp", "reg"), None, "tm", None),
            P(("inv", "rcp", "reg"), None),
            P(("inv", "rcp", "reg")),
            P(("inv", "rcp", "reg")),
            P("inv"),
        ),
        out_specs=P(("inv", "rcp"), None, ("reg", "tm")),
        check_vma=False,
    )
```

```python
import functools

import jax
import jax.numpy as jnp
from jax import lax
from jax.experimental import pallas as pl
from jax.experimental.pallas import tpu as pltpu
from jax.sharding import PartitionSpec as P

F32 = jnp.float32
BF16 = jnp.bfloat16
I32 = jnp.int32
META = 16
VMEM_LIMIT = 48 * 1024 * 1024
FORWARD_BYTES = 0


def up(x, m):
    return (x + m - 1) // m * m


def log2(x):
    assert x & (x - 1) == 0
    return x.bit_length() - 1


def iota(shape, axis):
    return lax.broadcasted_iota(I32, shape, axis)


def mask(cond):
    return jnp.where(cond, jnp.float32(1), jnp.float32(0))


def nt(a, b):
    return lax.dot_general(a, b, (((1,), (1,)), ((), ())), preferred_element_type=F32)


def nn(a, b):
    return lax.dot_general(a, b, (((1,), (0,)), ((), ())), preferred_element_type=F32)


def pack_kernel(cfg, where_ref, small_ref, fp_ref, *outs):
    n, capp, local_blocks, slots, w2 = cfg["n"], cfg["capp"], cfg["local"], cfg["slots"], cfg["w2"]
    receptors = cfg["receptors"]
    cols = receptors * slots * w2
    ids = small_ref.shape[1]
    at_place = receptors
    used = n * capp
    padded = up(used, 256)
    half = n // 2
    me = where_ref[0]
    tm = where_ref[1]
    lane = iota((1, cols), 1)
    entry = lane >> log2(w2)
    w_of = lane & (w2 - 1)
    s_of = entry & (slots - 1)
    r_of = entry >> log2(slots)
    sel_s = mask(iota((slots, cols), 0) == s_of).astype(BF16)
    sel_r = mask(iota((receptors, cols), 0) == r_of).astype(BF16)
    before = ((iota((cols, cols), 0) >> log2(w2)) < entry) & ((iota((cols, cols), 0) & (w2 - 1)) == 0)
    before = mask(before).astype(BF16)
    b = small_ref[0:receptors, 0:slots].astype(I32)
    high = (b >> 6).astype(F32).astype(BF16)
    low = (b & 63).astype(F32).astype(BF16)
    spread = nn(high, sel_s) * 64.0 + nn(low, sel_s)
    on_row = iota((receptors, cols), 0) == r_of
    geo = jnp.sum(jnp.where(on_row, spread, 0.0), axis=0, keepdims=True).astype(I32)
    place = small_ref[at_place : at_place + 1, :].astype(I32)
    row16 = iota((16, ids), 0)
    owner_tab = (place >> log2(local_blocks)).astype(F32)
    local_tab = (place & (local_blocks - 1)).astype(F32)
    tab = jnp.where(row16 == 0, owner_tab, jnp.where(row16 == 1, local_tab, 0.0)).astype(BF16)
    found = nn(tab, mask(iota((ids, cols), 0) == geo).astype(BF16))
    step = found[0:1].astype(I32) - me
    step = jnp.where(step < 0, step + n, step)
    local_row = found[1:2]
    to_owner = iota((up(n, 16), cols), 0) == step
    ranks = nn(mask(to_owner).astype(BF16), before)
    rank = jnp.sum(jnp.where(to_owner, ranks, 0.0), axis=0, keepdims=True).astype(I32)
    slot = step * capp + rank
    hour = small_ref[at_place + 1 : at_place + 2, 0:receptors]
    weight = small_ref[at_place + 2 : at_place + 3, 0:receptors]
    w_hi = weight.astype(BF16).astype(F32)
    w_mid = (weight - w_hi).astype(BF16).astype(F32)
    w_lo = weight - w_hi - w_mid
    row_r = iota((16, receptors), 0)
    per_r = jnp.where(row_r == 1, hour, 0.0)
    per_r = jnp.where(row_r == 3, w_hi, per_r)
    per_r = jnp.where(row_r == 4, w_mid, per_r)
    per_r = jnp.where(row_r == 5, w_lo, per_r)
    values = nn(per_r.astype(BF16), sel_r)
    row_m = iota((16, cols), 0)
    values = jnp.where(row_m == 0, local_row + 1.0, values)
    values = jnp.where(row_m == 1, values + (tm * w2).astype(F32), values)
    values = jnp.where(row_m == 2, (r_of + me * receptors).astype(F32), values)
    fp = fp_ref[...]
    for w in range(w2):
        slot_w = jnp.where(w_of == w, slot, -1)
        pick = mask(iota((padded, cols), 0) == slot_w).astype(BF16)
        moved = nn(pick, fp).astype(BF16)
        for d in range(n):
            outs[d][w * capp : (w + 1) * capp, :] = moved[d * capp : (d + 1) * capp]
        if w == 0:
            meta = nt(values.astype(BF16), pick)
            at = iota((16, half * capp), 1)
            for d in range(n):
                base = d // half * half * capp
                place_d = d % half * capp
                mine = meta[:, base : base + half * capp]
                mine = jnp.where((at >= place_d) & (at < place_d + capp), mine, 0.0).astype(BF16)
                outs[d][w2 * capp : w2 * capp + META, :] = jnp.zeros((META, outs[d].shape[1]), BF16)
                outs[d][w2 * capp : w2 * capp + META, 0 : half * capp] = mine


def pack(cfg, where, blocks, hour_start, obs_weight, placement, footprint):
    n, capp, slots, w2 = cfg["n"], cfg["capp"], cfg["slots"], cfg["w2"]
    receptors = blocks.shape[0]
    cells = footprint.shape[3]
    rows = w2 * capp + META
    ids = placement.shape[0]
    height = up(receptors + 3, 8)

    def put(x, at):
        return jnp.pad(x, ((at, height - at - x.shape[0]), (0, ids - x.shape[1])))

    small = put(blocks, 0) + put(placement[None], receptors) + put(hour_start[None], receptors + 1)
    small = small.astype(F32) + put(obs_weight[None], receptors + 2)
    vm = pl.BlockSpec(memory_space=pltpu.VMEM)
    return pl.pallas_call(
        functools.partial(pack_kernel, cfg),
        out_shape=[jax.ShapeDtypeStruct((rows, cells), BF16)] * n,
        in_specs=[pl.BlockSpec(memory_space=pltpu.SMEM), vm, vm],
        out_specs=[vm] * n,
        compiler_params=pltpu.CompilerParams(vmem_limit_bytes=VMEM_LIMIT),
        name="pack",
    )(where, small, footprint.reshape(receptors * slots * w2, cells))


def slots_of(bufs, rows):
    return [(buf, base) for buf in bufs for base in range(0, buf.shape[0], rows)]


def load_meta(cfg, placed):
    w2, capp = cfg["w2"], cfg["capp"]
    total = None
    for buf, base in placed:
        part = buf[base + w2 * capp : base + w2 * capp + META, :].astype(F32)
        total = part if total is None else total + part
    return total[:, 0 : len(placed) * capp]


def hour_column(meta, width):
    pick = mask(iota((16, width), 0) == 1)
    return lax.dot_general(
        meta.astype(BF16), pick.astype(BF16), (((0,), (0,)), ((), ())), preferred_element_type=F32
    )


def spread_hours(cfg, sides, metas, f8_ref, base_row):
    w2, capp, hours, cells = cfg["w2"], cfg["capp"], cfg["hours"], cfg["cells"]
    columns = [hour_column(m, cells).astype(BF16) for m in metas]
    for d in range(len(sides[0])):
        parts = []
        for side in range(len(sides)):
            buf, base = sides[side][d]
            first = columns[side][d * capp : (d + 1) * capp]
            for w in range(w2):
                parts.append((first + BF16(w) if w else first, buf[base + w * capp : base + (w + 1) * capp, :]))
        for h in range(hours):
            value = jnp.zeros((capp, cells), BF16)
            for first, fp in parts:
                value = jnp.where(first == BF16(h), fp, value)
            f8_ref[base_row + d * capp : base_row + (d + 1) * capp, h * cells : (h + 1) * cells] = value


def after_kernel(x_ref, unread_ref, out_ref):
    out_ref[...] = x_ref[...]


def after(x, first):
    return pl.pallas_call(
        after_kernel,
        out_shape=jax.ShapeDtypeStruct(x.shape, x.dtype),
        grid=(1,),
        in_specs=[pl.BlockSpec(x.shape, lambda i: (0, 0)), pl.BlockSpec((16, 128), lambda i: (0, 0))],
        out_specs=pl.BlockSpec(x.shape, lambda i: (0, 0)),
        compiler_params=pltpu.CompilerParams(vmem_limit_bytes=4 * 1024 * 1024),
        cost_estimate=pl.CostEstimate(flops=0, bytes_accessed=2 * x.size, transcendentals=0),
        name="after",
    )(x, first)


def stack_kernel(count, *refs):
    out_ref, at = refs[-1], 0
    for ref in refs[:count]:
        out_ref[at : at + ref.shape[0], :] = ref[...]
        at += ref.shape[0]


def stack(bufs, *unread):
    vm = pl.BlockSpec(memory_space=pltpu.VMEM)
    rows = sum(b.shape[0] for b in bufs)
    return pl.pallas_call(
        functools.partial(stack_kernel, len(bufs)),
        out_shape=jax.ShapeDtypeStruct((rows, bufs[0].shape[1]), BF16),
        in_specs=[vm] * (len(bufs) + len(unread)),
        out_specs=vm,
        compiler_params=pltpu.CompilerParams(vmem_limit_bytes=16 * 1024 * 1024),
        cost_estimate=pl.CostEstimate(flops=0, bytes_accessed=0, transcendentals=0),
        name="stack",
    )(*bufs, *unread)


def forward_kernel(cfg, counts, *refs):
    local, k, rows, capp = cfg["local"], cfg["k_core"], cfg["rows"], cfg["capp"]
    half = cfg["n"] // 2 * capp
    out_ref, f8_ref = refs[-2:]
    at = 0
    firsts = []
    for i, sides_n in enumerate(counts):
        sides = []
        for count in sides_n:
            sides.append(slots_of(refs[at : at + count], rows))
            at += count
        metas = [load_meta(cfg, placed) for placed in sides]
        spread_hours(cfg, sides, metas, f8_ref, i * half)
        firsts.append(metas[0][0:8])
    probes_ref = refs[at]
    meta = jnp.concatenate(firsts, axis=1)
    used = meta.shape[1]
    own = iota((local, used), 0) + 1 == meta[0:1].astype(I32)
    row = iota((8, used), 0)
    dots = jnp.zeros((8, used), F32)
    f8 = f8_ref[...]
    for j in range(k):
        x = nt(probes_ref[j * local : (j + 1) * local, :], f8)
        y = jnp.sum(jnp.where(own, x, 0.0), axis=0, keepdims=True)
        dots = jnp.where(row == j, y, dots)
    to_r = mask(iota((out_ref.shape[1], used), 0) == meta[2:3].astype(I32))
    out_ref[...] = lax.dot_general(
        dots, to_r, (((1,), (1,)), ((), ())), precision=lax.Precision.HIGHEST, preferred_element_type=F32
    )


def forward(cfg, own, probes_t, out_shape, unread):
    n, capp, hours, cells = cfg["n"], cfg["capp"], cfg["hours"], cfg["cells"]
    args = [b for half in own for side in half for b in side]
    counts = [[len(side) for side in half] for half in own]
    vm = pl.BlockSpec(memory_space=pltpu.VMEM)
    return pl.pallas_call(
        functools.partial(forward_kernel, cfg, counts),
        out_shape=jax.ShapeDtypeStruct(out_shape, F32),
        in_specs=[vm] * (len(args) + 1) + [pl.BlockSpec(memory_space=pl.ANY)] * len(unread),
        out_specs=vm,
        scratch_shapes=[pltpu.VMEM((n * capp, hours * cells), BF16)],
        compiler_params=pltpu.CompilerParams(vmem_limit_bytes=VMEM_LIMIT),
        cost_estimate=pl.CostEstimate(flops=0, bytes_accessed=FORWARD_BYTES, transcendentals=0),
        name="forward",
    )(*args, probes_t, *unread)


def prepare_kernel(cfg, counts, *refs):
    n, capp = cfg["n"], cfg["capp"]
    f8_ref, meta_ref = refs[-2:]
    at = 0
    for c, halves in enumerate(counts):
        metas = []
        whole = [[] for _ in halves[0]]
        for sides_n in halves:
            for side, count in enumerate(sides_n):
                whole[side] += slots_of(refs[at : at + count], cfg["rows"])
                at += count
        for i in range(2):
            sides = [side[i * n // 2 : (i + 1) * n // 2] for side in whole]
            side_metas = [load_meta(cfg, placed) for placed in sides]
            spread_hours(cfg, sides, side_metas, f8_ref, (2 * c + i) * (n // 2) * capp)
            metas.append(side_metas[0][0:8])
        meta_ref[:, c * n * capp : (c + 1) * n * capp] = jnp.concatenate(metas, axis=1)


def prepare(cfg, columns):
    n, capp, hours, cells = cfg["n"], cfg["capp"], cfg["hours"], cfg["cells"]
    total = len(columns) * n * capp
    args = [b for halves in columns for sides in halves for side in sides for b in side]
    counts = [[[len(side) for side in sides] for sides in halves] for halves in columns]
    vm = pl.BlockSpec(memory_space=pltpu.VMEM)
    return pl.pallas_call(
        functools.partial(prepare_kernel, cfg, counts),
        out_shape=[
            jax.ShapeDtypeStruct((total, hours * cells), BF16),
            jax.ShapeDtypeStruct((8, total), F32),
        ],
        in_specs=[vm] * len(args),
        out_specs=[vm] * 2,
        compiler_params=pltpu.CompilerParams(vmem_limit_bytes=VMEM_LIMIT),
        cost_estimate=pl.CostEstimate(flops=0, bytes_accessed=6 * total * hours * cells, transcendentals=0),
        name="prepare",
    )(*args)


def adjoint_kernel(cfg, parts, where_ref, meta_ref, f8_ref, *refs):
    n, capp, local, hours, cells, kd = (
        cfg["n"], cfg["capp"], cfg["local"], cfg["hours"], cfg["cells"], cfg["kd"],
    )
    obs_refs, (out_ref, a_ref, tiles_ref, sems) = refs[:-4], refs[-4:]
    used = n * capp
    per_k = cells // 128
    for c in range(len(obs_refs) // parts):
        obs = obs_refs[c * parts][...]
        for i in range(1, parts):
            obs = obs + obs_refs[c * parts + i][...]
        meta = meta_ref[:, c * used : (c + 1) * used]
        to_r = mask(iota((obs.shape[1], used), 0) == meta[2:3].astype(I32))
        per_entry = lax.dot_general(
            obs, to_r, (((1,), (0,)), ((), ())), precision=lax.Precision.HIGHEST, preferred_element_type=F32
        )
        per_entry = per_entry * (meta[3:4] + meta[4:5] + meta[5:6])
        own = iota((local, used), 0) + 1 == meta[0:1].astype(I32)
        row = iota((8, used), 0)
        for j in range(kd):
            term = jnp.sum(jnp.where(row == where_ref[2] * kd + j, per_entry, 0.0), axis=0, keepdims=True)
            high = term.astype(BF16).astype(F32)
            for p, part in enumerate((high, term - high)):
                a_ref[(2 * j + p) * local : (2 * j + p + 1) * local, c * used : (c + 1) * used] = jnp.where(
                    own, part, 0.0
                ).astype(BF16)
    copies = []
    for j in range(kd):
        a = a_ref[2 * j * local : 2 * (j + 1) * local, :]
        for h in range(hours):
            sums = nn(a, f8_ref[:, h * cells : (h + 1) * cells])
            both = sums[0:local] + sums[local : 2 * local]
            for t in range(per_k):
                tiles_ref.at[j * per_k + t][pl.ds(h, local, stride=hours), :] = both[:, t * 128 : (t + 1) * 128]
        for t in range(j * per_k, (j + 1) * per_k):
            copy = pltpu.make_async_copy(tiles_ref.at[t], out_ref.at[:, pl.ds(t * 128, 128)], sems.at[t])
            copy.start()
            copies.append(copy)
    for copy in copies:
        copy.wait()


def adjoint(cfg, where, f8, meta, observed):
    hours, cells, local, kd = cfg["hours"], cfg["cells"], cfg["local"], cfg["kd"]
    total = f8.shape[0]
    parts = len(observed[0])
    args = [o for column in observed for o in column]
    vm = pl.BlockSpec(memory_space=pltpu.VMEM)
    return pl.pallas_call(
        functools.partial(adjoint_kernel, cfg, parts),
        out_shape=jax.ShapeDtypeStruct((local * hours, kd * cells), F32),
        in_specs=[pl.BlockSpec(memory_space=pltpu.SMEM)] + [vm] * (2 + len(args)),
        out_specs=pl.BlockSpec(memory_space=pl.ANY),
        scratch_shapes=[
            pltpu.VMEM((2 * kd * local, total), BF16),
            pltpu.VMEM((kd * cells // 128, local * hours, 128), F32),
            pltpu.SemaphoreType.DMA((kd * cells // 128,)),
        ],
        compiler_params=pltpu.CompilerParams(vmem_limit_bytes=VMEM_LIMIT),
        name="adjoint",
    )(where, meta, f8, *args)


def shift(x, axis, d):
    n = lax.axis_size(axis)
    return lax.ppermute(x, axis, [(i, (i + d) % n) for i in range(n)])


def shards(probes, footprint, blocks, hour_start, obs_weight, placement):
    n, nreg, ntm = lax.axis_size("rcp"), lax.axis_size("reg"), lax.axis_size("tm")
    local, hours, width = probes.shape
    receptors, slots, w2, cells = footprint.shape
    k = width // cells
    kd = k // (nreg * ntm)
    capp = up(3 * receptors * slots // (2 * n), 16)
    cfg = dict(
        n=n, capp=capp, local=local, hours=hours, cells=cells, receptors=receptors, slots=slots, w2=w2,
        kd=kd, k_core=nreg * kd, rows=w2 * capp + META,
    )
    z, reg, tm = lax.axis_index("rcp"), lax.axis_index("reg"), lax.axis_index("tm")
    where = jnp.stack([z, tm, reg]).astype(I32)
    outs = pack(cfg, where, blocks, hour_start, obs_weight, placement, footprint)
    probes_t = lax.dynamic_index_in_dim(probes.reshape(local, hours, nreg, ntm, kd, cells), tm, 3, keepdims=False)
    probes_t = probes_t.transpose(2, 3, 0, 1, 4).reshape(nreg * kd * local, hours * cells)

    def with_cores(half):
        return [half] + [[shift(b, "tm", s) for b in half] for s in range(1, ntm)]

    mine = after(outs[0], probes_t)
    arrived = [shift(outs[d], "rcp", d) for d in range(1, n)]
    bufs = [mine] + arrived
    halves = [bufs[: n // 2], bufs[n // 2 :]]
    if n > 4:
        halves = [[jnp.concatenate(half, axis=0)] for half in halves]
    own = [with_cores(half) for half in halves]
    others = stack(arrived)
    first = [shift(mine, "reg", g) for g in range(1, nreg)]
    partial = forward(cfg, own, probes_t, (8, up(n * receptors, 128)), first)
    second = [shift(others, "reg", g) for g in range(1, nreg)]
    observed = partial
    for d in range(1, n):
        observed = observed + shift(partial, "rcp", d)
    columns = [own]
    for g in range(1, nreg):
        across = stack([first[g - 1], second[g - 1]], observed)
        columns.append([with_cores([across])])
    f8, meta = prepare(cfg, columns)
    observed = [[shift(observed, "reg", g) if g else observed] for g in range(nreg)]
    result = adjoint(cfg, where, f8, meta, observed)
    return result.reshape(local, hours, kd * cells)


def solution(mesh):
    return jax.shard_map(
        shards,
        mesh=mesh,
        in_specs=(
            P(("inv", "rcp"), None, None),
            P(("inv", "rcp", "reg"), None, "tm", None),
            P(("inv", "rcp", "reg"), None),
            P(("inv", "rcp", "reg")),
            P(("inv", "rcp", "reg")),
            P("inv"),
        ),
        out_specs=P(("inv", "rcp"), None, ("reg", "tm")),
        check_vma=False,
    )
```

```python
import functools

import jax
import jax.numpy as jnp
from jax import lax
from jax.experimental import pallas as pl
from jax.experimental.pallas import tpu as pltpu
from jax.sharding import PartitionSpec as P

F32 = jnp.float32
BF16 = jnp.bfloat16
I32 = jnp.int32
META = 16
VMEM_LIMIT = 48 * 1024 * 1024
GROUPS = ((0,), (1, 2, 3))
EARLY = 0
FORWARD_BYTES = 0


def up(x, m):
    return (x + m - 1) // m * m


def log2(x):
    assert x & (x - 1) == 0
    return x.bit_length() - 1


def iota(shape, axis):
    return lax.broadcasted_iota(I32, shape, axis)


def mask(cond):
    return jnp.where(cond, jnp.float32(1), jnp.float32(0))


def nt(a, b):
    return lax.dot_general(a, b, (((1,), (1,)), ((), ())), preferred_element_type=F32)


def nn(a, b):
    return lax.dot_general(a, b, (((1,), (0,)), ((), ())), preferred_element_type=F32)


def three(x):
    high = x.astype(BF16).astype(F32)
    mid = (x - high).astype(BF16).astype(F32)
    return jnp.concatenate([high, mid, x - high - mid], axis=0).astype(BF16)


def add_three(x):
    rows = x.shape[0] // 3
    return x[0:rows] + x[rows : 2 * rows] + x[2 * rows : 3 * rows]


def pack_kernel(cfg, where_ref, small_ref, fp_ref, *outs):
    n, capp, local_blocks, slots, w2 = cfg["n"], cfg["capp"], cfg["local"], cfg["slots"], cfg["w2"]
    receptors = cfg["receptors"]
    cols = receptors * slots * w2
    ids = small_ref.shape[1]
    at_place = receptors
    used = n * capp
    padded = up(used, 256)
    half = n // 2
    me = where_ref[0]
    tm = where_ref[1]
    lane = iota((1, cols), 1)
    entry = lane >> log2(w2)
    w_of = lane & (w2 - 1)
    s_of = entry & (slots - 1)
    r_of = entry >> log2(slots)
    sel_s = mask(iota((slots, cols), 0) == s_of).astype(BF16)
    sel_r = mask(iota((receptors, cols), 0) == r_of).astype(BF16)
    before = ((iota((cols, cols), 0) >> log2(w2)) < entry) & ((iota((cols, cols), 0) & (w2 - 1)) == 0)
    before = mask(before).astype(BF16)
    b = small_ref[0:receptors, 0:slots].astype(I32)
    high = (b >> 6).astype(F32).astype(BF16)
    low = (b & 63).astype(F32).astype(BF16)
    spread = nn(high, sel_s) * 64.0 + nn(low, sel_s)
    on_row = iota((receptors, cols), 0) == r_of
    geo = jnp.sum(jnp.where(on_row, spread, 0.0), axis=0, keepdims=True).astype(I32)
    place = small_ref[at_place : at_place + 1, :].astype(I32)
    row16 = iota((16, ids), 0)
    owner_tab = (place >> log2(local_blocks)).astype(F32)
    local_tab = (place & (local_blocks - 1)).astype(F32)
    tab = jnp.where(row16 == 0, owner_tab, jnp.where(row16 == 1, local_tab, 0.0)).astype(BF16)
    found = nn(tab, mask(iota((ids, cols), 0) == geo).astype(BF16))
    step = found[0:1].astype(I32) - me
    step = jnp.where(step < 0, step + n, step)
    local_row = found[1:2]
    to_owner = iota((up(n, 16), cols), 0) == step
    ranks = nn(mask(to_owner).astype(BF16), before)
    rank = jnp.sum(jnp.where(to_owner, ranks, 0.0), axis=0, keepdims=True).astype(I32)
    slot = step * capp + rank
    hour = small_ref[at_place + 1 : at_place + 2, 0:receptors]
    weight = small_ref[at_place + 2 : at_place + 3, 0:receptors]
    w_hi = weight.astype(BF16).astype(F32)
    w_mid = (weight - w_hi).astype(BF16).astype(F32)
    w_lo = weight - w_hi - w_mid
    row_r = iota((16, receptors), 0)
    per_r = jnp.where(row_r == 1, hour, 0.0)
    per_r = jnp.where(row_r == 3, w_hi, per_r)
    per_r = jnp.where(row_r == 4, w_mid, per_r)
    per_r = jnp.where(row_r == 5, w_lo, per_r)
    values = nn(per_r.astype(BF16), sel_r)
    row_m = iota((16, cols), 0)
    values = jnp.where(row_m == 0, local_row + 1.0, values)
    values = jnp.where(row_m == 1, values + (tm * w2).astype(F32), values)
    values = jnp.where(row_m == 2, (r_of + me * receptors).astype(F32), values)
    fp = fp_ref[...]
    for w in range(w2):
        slot_w = jnp.where(w_of == w, slot, -1)
        pick = mask(iota((padded, cols), 0) == slot_w).astype(BF16)
        moved = nn(pick, fp).astype(BF16)
        for d in range(n):
            outs[d][w * capp : (w + 1) * capp, :] = moved[d * capp : (d + 1) * capp]
        if w == 0:
            meta = nt(values.astype(BF16), pick)
            at = iota((16, half * capp), 1)
            for d in range(n):
                base = d // half * half * capp
                place_d = d % half * capp
                mine = meta[:, base : base + half * capp]
                mine = jnp.where((at >= place_d) & (at < place_d + capp), mine, 0.0).astype(BF16)
                outs[d][w2 * capp : w2 * capp + META, :] = jnp.zeros((META, outs[d].shape[1]), BF16)
                outs[d][w2 * capp : w2 * capp + META, 0 : half * capp] = mine


def pack(cfg, where, blocks, hour_start, obs_weight, placement, footprint):
    n, capp, slots, w2 = cfg["n"], cfg["capp"], cfg["slots"], cfg["w2"]
    receptors = blocks.shape[0]
    cells = footprint.shape[3]
    rows = w2 * capp + META
    ids = placement.shape[0]
    height = up(receptors + 3, 8)

    def put(x, at):
        return jnp.pad(x, ((at, height - at - x.shape[0]), (0, ids - x.shape[1])))

    small = put(blocks, 0) + put(placement[None], receptors) + put(hour_start[None], receptors + 1)
    small = small.astype(F32) + put(obs_weight[None], receptors + 2)
    vm = pl.BlockSpec(memory_space=pltpu.VMEM)
    return pl.pallas_call(
        functools.partial(pack_kernel, cfg),
        out_shape=[jax.ShapeDtypeStruct((rows, cells), BF16)] * n,
        in_specs=[pl.BlockSpec(memory_space=pltpu.SMEM), vm, vm],
        out_specs=[vm] * n,
        compiler_params=pltpu.CompilerParams(vmem_limit_bytes=VMEM_LIMIT),
        name="pack",
    )(where, small, footprint.reshape(receptors * slots * w2, cells))


def slots_of(bufs, rows):
    return [(buf, base) for buf in bufs for base in range(0, buf.shape[0], rows)]


def load_meta(cfg, placed):
    w2, capp = cfg["w2"], cfg["capp"]
    total = None
    for buf, base in placed:
        part = buf[base + w2 * capp : base + w2 * capp + META, :].astype(F32)
        total = part if total is None else total + part
    return total[:, 0 : len(placed) * capp]


def hour_column(meta, width):
    pick = mask(iota((16, width), 0) == 1)
    return lax.dot_general(
        meta.astype(BF16), pick.astype(BF16), (((0,), (0,)), ((), ())), preferred_element_type=F32
    )


def spread_hours(cfg, sides, metas, f8_ref, base_row):
    w2, capp, hours, cells = cfg["w2"], cfg["capp"], cfg["hours"], cfg["cells"]
    columns = [hour_column(m, cells).astype(BF16) for m in metas]
    for d in range(len(sides[0])):
        parts = []
        for side in range(len(sides)):
            buf, base = sides[side][d]
            first = columns[side][d * capp : (d + 1) * capp]
            for w in range(w2):
                parts.append((first + BF16(w) if w else first, buf[base + w * capp : base + (w + 1) * capp, :]))
        for h in range(hours):
            value = jnp.zeros((capp, cells), BF16)
            for first, fp in parts:
                value = jnp.where(first == BF16(h), fp, value)
            f8_ref[base_row + d * capp : base_row + (d + 1) * capp, h * cells : (h + 1) * cells] = value


def after_kernel(x_ref, unread_ref, out_ref):
    out_ref[...] = x_ref[...]


def after(x, first):
    return pl.pallas_call(
        after_kernel,
        out_shape=jax.ShapeDtypeStruct(x.shape, x.dtype),
        grid=(1,),
        in_specs=[pl.BlockSpec(x.shape, lambda i: (0, 0)), pl.BlockSpec((16, 128), lambda i: (0, 0))],
        out_specs=pl.BlockSpec(x.shape, lambda i: (0, 0)),
        compiler_params=pltpu.CompilerParams(vmem_limit_bytes=4 * 1024 * 1024),
        cost_estimate=pl.CostEstimate(flops=0, bytes_accessed=2 * x.size, transcendentals=0),
        name="after",
    )(x, first)


def stack_kernel(count, *refs):
    out_ref, at = refs[-1], 0
    for ref in refs[:count]:
        out_ref[at : at + ref.shape[0], :] = ref[...]
        at += ref.shape[0]


def stack(bufs, *unread):
    vm = pl.BlockSpec(memory_space=pltpu.VMEM)
    rows = sum(b.shape[0] for b in bufs)
    return pl.pallas_call(
        functools.partial(stack_kernel, len(bufs)),
        out_shape=jax.ShapeDtypeStruct((rows, bufs[0].shape[1]), BF16),
        in_specs=[vm] * (len(bufs) + len(unread)),
        out_specs=vm,
        compiler_params=pltpu.CompilerParams(vmem_limit_bytes=16 * 1024 * 1024),
        cost_estimate=pl.CostEstimate(flops=0, bytes_accessed=0, transcendentals=0),
        name="stack",
    )(*bufs, *unread)


def forward_kernel(cfg, counts, *refs):
    local, k, rows, capp = cfg["local"], cfg["k_core"], cfg["rows"], cfg["capp"]
    half = cfg["n"] // 2 * capp
    out_ref, f8_ref = refs[-2:]
    at = 0
    firsts = []
    for i, sides_n in enumerate(counts):
        sides = []
        for count in sides_n:
            sides.append(slots_of(refs[at : at + count], rows))
            at += count
        metas = [load_meta(cfg, placed) for placed in sides]
        spread_hours(cfg, sides, metas, f8_ref, i * half)
        firsts.append(metas[0][0:8])
    probes_ref = refs[at]
    meta = jnp.concatenate(firsts, axis=1)
    used = meta.shape[1]
    own = iota((local, used), 0) + 1 == meta[0:1].astype(I32)
    row = iota((8, used), 0)
    dots = jnp.zeros((8, used), F32)
    f8 = f8_ref[...]
    x = nt(probes_ref[...], f8)
    for j in range(k):
        y = jnp.sum(jnp.where(own, x[j * local : (j + 1) * local], 0.0), axis=0, keepdims=True)
        dots = jnp.where(row == j, y, dots)
    to_r = mask(iota((out_ref.shape[1], used), 0) == meta[2:3].astype(I32)).astype(BF16)
    out_ref[...] = add_three(nt(three(dots), to_r))


def forward(cfg, own, probes_t, out_shape, unread):
    n, capp, hours, cells = cfg["n"], cfg["capp"], cfg["hours"], cfg["cells"]
    args = [b for half in own for side in half for b in side]
    counts = [[len(side) for side in half] for half in own]
    vm = pl.BlockSpec(memory_space=pltpu.VMEM)
    return pl.pallas_call(
        functools.partial(forward_kernel, cfg, counts),
        out_shape=jax.ShapeDtypeStruct(out_shape, F32),
        in_specs=[vm] * (len(args) + 1) + [pl.BlockSpec(memory_space=pl.ANY)] * len(unread),
        out_specs=vm,
        scratch_shapes=[pltpu.VMEM((n * capp, hours * cells), BF16)],
        compiler_params=pltpu.CompilerParams(vmem_limit_bytes=VMEM_LIMIT),
        cost_estimate=pl.CostEstimate(flops=0, bytes_accessed=FORWARD_BYTES, transcendentals=0),
        name="forward",
    )(*args, probes_t, *unread)


def prepare_kernel(cfg, column, counts, *refs):
    n, capp, local = cfg["n"], cfg["capp"], cfg["local"]
    f8_ref, own_ref, to_r_ref, weight_ref = refs[-4:]
    used = n * capp
    at = 0
    whole = [[] for _ in counts[0]]
    for sides_n in counts:
        for side, count in enumerate(sides_n):
            whole[side] += slots_of(refs[at : at + count], cfg["rows"])
            at += count
    firsts = []
    for i in range(2):
        sides = [side[i * n // 2 : (i + 1) * n // 2] for side in whole]
        metas = [load_meta(cfg, placed) for placed in sides]
        spread_hours(cfg, sides, metas, f8_ref, column * used + i * (n // 2) * capp)
        firsts.append(metas[0][0:8])
    meta = jnp.concatenate(firsts, axis=1)
    lanes = slice(column * used, (column + 1) * used)
    own_ref[:, lanes] = mask(iota((local, used), 0) + 1 == meta[0:1].astype(I32)).astype(BF16)
    to_r_ref[:, lanes] = mask(iota((to_r_ref.shape[0], used), 0) == meta[2:3].astype(I32)).astype(BF16)
    weight_ref[:, lanes] = jnp.broadcast_to(meta[3:4] + meta[4:5] + meta[5:6], (8, used))


def prepare(cfg, column, halves, columns, rp, before, *unread):
    n, capp, hours, cells, local = cfg["n"], cfg["capp"], cfg["hours"], cfg["cells"], cfg["local"]
    total = columns * n * capp
    args = [b for sides in halves for side in sides for b in side]
    counts = [[len(side) for side in sides] for sides in halves]
    vm = pl.BlockSpec(memory_space=pltpu.VMEM)
    return pl.pallas_call(
        functools.partial(prepare_kernel, cfg, column, counts),
        out_shape=[
            jax.ShapeDtypeStruct((total, hours * cells), BF16),
            jax.ShapeDtypeStruct((local, total), BF16),
            jax.ShapeDtypeStruct((rp, total), BF16),
            jax.ShapeDtypeStruct((8, total), F32),
        ],
        in_specs=[vm] * (len(args) + len(before) + len(unread)),
        out_specs=[vm] * 4,
        input_output_aliases={len(args) + i: i for i in range(len(before))},
        compiler_params=pltpu.CompilerParams(vmem_limit_bytes=VMEM_LIMIT),
        cost_estimate=pl.CostEstimate(flops=0, bytes_accessed=3 * total * cells, transcendentals=0),
        name=f"prepare{column}",
    )(*args, *before, *unread)


def fill_terms(cfg, reg, obs_ref, own, to_r, weight, a_ref, lanes):
    local, kd = cfg["local"], cfg["kd"]
    used = own.shape[1]
    row = iota((8, used), 0)
    per_entry = add_three(nn(three(obs_ref[...]), to_r)) * weight
    for j in range(kd):
        term = jnp.sum(jnp.where(row == reg * kd + j, per_entry, 0.0), axis=0, keepdims=True)
        high = term.astype(BF16).astype(F32)
        for p, part in enumerate((high, term - high)):
            spread = jnp.broadcast_to(part.astype(BF16), (local, used))
            a_ref[(2 * j + p) * local : (2 * j + p + 1) * local, lanes] = own * spread


def own_adjoint_kernel(cfg, where_ref, f8_ref, own_ref, to_r_ref, weight_ref, obs_ref, out_ref, a_ref):
    local, hours, cells, kd = cfg["local"], cfg["hours"], cfg["cells"], cfg["kd"]
    fill_terms(cfg, where_ref[2], obs_ref, own_ref[...], to_r_ref[...], weight_ref[...], a_ref, slice(None))
    a = a_ref[...]
    for h in range(hours):
        sums = nn(a, f8_ref[:, h * cells : (h + 1) * cells])
        for j in range(kd):
            both = sums[2 * j * local : (2 * j + 1) * local] + sums[(2 * j + 1) * local : (2 * j + 2) * local]
            out_ref[j * local : (j + 1) * local, h * cells : (h + 1) * cells] = both


def own_adjoint(cfg, where, operands, observed):
    hours, cells, local, kd = cfg["hours"], cfg["cells"], cfg["local"], cfg["kd"]
    total = operands[0].shape[0]
    vm = pl.BlockSpec(memory_space=pltpu.VMEM)
    return pl.pallas_call(
        functools.partial(own_adjoint_kernel, cfg),
        out_shape=jax.ShapeDtypeStruct((kd * local, hours * cells), F32),
        in_specs=[pl.BlockSpec(memory_space=pltpu.SMEM)] + [vm] * 5,
        out_specs=vm,
        scratch_shapes=[pltpu.VMEM((2 * kd * local, total), BF16)],
        compiler_params=pltpu.CompilerParams(vmem_limit_bytes=VMEM_LIMIT),
        cost_estimate=pl.CostEstimate(
            flops=4 * kd * local * total * hours * cells, bytes_accessed=2 * total * hours * cells, transcendentals=0
        ),
        name="own_adjoint",
    )(where, *operands, observed)


def adjoint_kernel(cfg, where_ref, before_ref, f8_ref, own_ref, to_r_ref, weight_ref, *refs):
    n, capp, local, hours, cells, kd = (
        cfg["n"], cfg["capp"], cfg["local"], cfg["hours"], cfg["cells"], cfg["kd"],
    )
    obs_refs, (out_ref, a_ref, tiles_ref, sems) = refs[:-4], refs[-4:]
    used = n * capp
    per_k = cells // 128
    for c, obs_ref in enumerate(obs_refs):
        lanes = slice(c * used, (c + 1) * used)
        fill_terms(
            cfg, where_ref[2], obs_ref, own_ref[:, lanes], to_r_ref[:, lanes], weight_ref[:, lanes], a_ref, lanes
        )
    copies = []
    for j in range(kd):
        a = a_ref[2 * j * local : 2 * (j + 1) * local, :]
        for h in range(hours):
            sums = nn(a, f8_ref[:, h * cells : (h + 1) * cells])
            both = sums[0:local] + sums[local : 2 * local]
            both = both + before_ref[j * local : (j + 1) * local, h * cells : (h + 1) * cells]
            for t in range(per_k):
                tiles_ref.at[j * per_k + t][pl.ds(h, local, stride=hours), :] = both[:, t * 128 : (t + 1) * 128]
        for t in range(j * per_k, (j + 1) * per_k):
            copy = pltpu.make_async_copy(tiles_ref.at[t], out_ref.at[:, pl.ds(t * 128, 128)], sems.at[t])
            copy.start()
            copies.append(copy)
    for copy in copies:
        copy.wait()


def adjoint(cfg, where, before, operands, observed):
    hours, cells, local, kd = cfg["hours"], cfg["cells"], cfg["local"], cfg["kd"]
    total = operands[0].shape[0]
    vm = pl.BlockSpec(memory_space=pltpu.VMEM)
    return pl.pallas_call(
        functools.partial(adjoint_kernel, cfg),
        out_shape=jax.ShapeDtypeStruct((local * hours, kd * cells), F32),
        in_specs=[pl.BlockSpec(memory_space=pltpu.SMEM)] + [vm] * (5 + len(observed)),
        out_specs=pl.BlockSpec(memory_space=pl.ANY),
        scratch_shapes=[
            pltpu.VMEM((2 * kd * local, total), BF16),
            pltpu.VMEM((kd * cells // 128, local * hours, 128), F32),
            pltpu.SemaphoreType.DMA((kd * cells // 128,)),
        ],
        compiler_params=pltpu.CompilerParams(vmem_limit_bytes=VMEM_LIMIT),
        name="adjoint",
    )(where, before, *operands, *observed)


def shift(x, axis, d):
    n = lax.axis_size(axis)
    return lax.ppermute(x, axis, [(i, (i + d) % n) for i in range(n)])


def shards(probes, footprint, blocks, hour_start, obs_weight, placement):
    n, nreg, ntm = lax.axis_size("rcp"), lax.axis_size("reg"), lax.axis_size("tm")
    local, hours, width = probes.shape
    receptors, slots, w2, cells = footprint.shape
    k = width // cells
    kd = k // (nreg * ntm)
    capp = up(3 * receptors * slots // (2 * n), 16)
    cfg = dict(
        n=n, capp=capp, local=local, hours=hours, cells=cells, receptors=receptors, slots=slots, w2=w2,
        kd=kd, k_core=nreg * kd, rows=w2 * capp + META,
    )
    z, reg, tm = lax.axis_index("rcp"), lax.axis_index("reg"), lax.axis_index("tm")
    where = jnp.stack([z, tm, reg]).astype(I32)
    outs = pack(cfg, where, blocks, hour_start, obs_weight, placement, footprint)
    probes_t = lax.dynamic_index_in_dim(probes.reshape(local, hours, nreg, ntm, kd, cells), tm, 3, keepdims=False)
    probes_t = probes_t.transpose(2, 3, 0, 1, 4).reshape(nreg * kd * local, hours * cells)

    def with_cores(half):
        return [half] + [[shift(b, "tm", s) for b in half] for s in range(1, ntm)]

    mine = after(outs[0], probes_t)
    bufs = [mine] + [shift(outs[d], "rcp", d) for d in range(1, n)]
    raw = [outs[0]] + bufs[1:]
    halves = [bufs[: n // 2], bufs[n // 2 :]]
    groups = GROUPS
    if n > 4:
        halves = [[jnp.concatenate(half, axis=0)] for half in halves]
        raw, groups = [half[0] for half in halves], ((0,), (1,))
    own = [with_cores(half) for half in halves]
    sent = [stack([raw[d] for d in group]) if len(group) > 1 else raw[group[0]] for group in groups]
    across = [[shift(b, "reg", g) for b in sent] for g in range(1, nreg)]
    rp = up(n * receptors, 128)
    partial = forward(cfg, own, probes_t, (8, rp), [b for group in across for b in group[:EARLY]])
    observed = partial
    for d in range(1, n):
        observed = observed + shift(partial, "rcp", d)
    operands = prepare(cfg, 0, own, 1, rp, [], partial)
    before = own_adjoint(cfg, where, operands, observed)
    gate, operands = operands[3], []
    for g, group in enumerate(across):
        group = stack(group, observed, gate)
        operands = prepare(cfg, g, [with_cores([group])], nreg - 1, rp, operands)
    observed = [shift(observed, "reg", g) for g in range(1, nreg)]
    result = adjoint(cfg, where, before, operands, observed)
    return result.reshape(local, hours, kd * cells)


def solution(mesh):
    return jax.shard_map(
        shards,
        mesh=mesh,
        in_specs=(
            P(("inv", "rcp"), None, None),
            P(("inv", "rcp", "reg"), None, "tm", None),
            P(("inv", "rcp", "reg"), None),
            P(("inv", "rcp", "reg")),
            P(("inv", "rcp", "reg")),
            P("inv"),
        ),
        out_specs=P(("inv", "rcp"), None, ("reg", "tm")),
        check_vma=False,
    )
```

```python
import functools

import jax
import jax.numpy as jnp
from jax import lax
from jax.experimental import pallas as pl
from jax.experimental.pallas import tpu as pltpu
from jax.sharding import PartitionSpec as P

F32 = jnp.float32
BF16 = jnp.bfloat16
I32 = jnp.int32
QUARTERS = 4
META = 16
VMEM_LIMIT = 48 * 1024 * 1024
GROUPS = ((0,), (1, 2, 3))
EARLY = 1
FORWARD_BYTES = 0


def up(x, m):
    return (x + m - 1) // m * m


def log2(x):
    assert x & (x - 1) == 0
    return x.bit_length() - 1


def iota(shape, axis):
    return lax.broadcasted_iota(I32, shape, axis)


def mask(cond):
    return jnp.where(cond, jnp.float32(1), jnp.float32(0))


def nt(a, b):
    return lax.dot_general(a, b, (((1,), (1,)), ((), ())), preferred_element_type=F32)


def nn(a, b):
    return lax.dot_general(a, b, (((1,), (0,)), ((), ())), preferred_element_type=F32)


def three(x):
    high = x.astype(BF16).astype(F32)
    mid = (x - high).astype(BF16).astype(F32)
    return jnp.concatenate([high, mid, x - high - mid], axis=0).astype(BF16)


def add_three(x):
    rows = x.shape[0] // 3
    return x[0:rows] + x[rows : 2 * rows] + x[2 * rows : 3 * rows]


def pack_kernel(cfg, where_ref, small_ref, fp_ref, *outs):
    n, capp, local_blocks, slots, w2 = cfg["n"], cfg["capp"], cfg["local"], cfg["slots"], cfg["w2"]
    receptors = cfg["receptors"]
    cols = receptors * slots * w2
    ids = small_ref.shape[1]
    at_place = receptors
    used = n * capp
    padded = up(used, 256)
    half = n // 2
    me = where_ref[0]
    tm = where_ref[1]
    lane = iota((1, cols), 1)
    entry = lane >> log2(w2)
    w_of = lane & (w2 - 1)
    s_of = entry & (slots - 1)
    r_of = entry >> log2(slots)
    sel_s = mask(iota((slots, cols), 0) == s_of).astype(BF16)
    sel_r = mask(iota((receptors, cols), 0) == r_of).astype(BF16)
    before = ((iota((cols, cols), 0) >> log2(w2)) < entry) & ((iota((cols, cols), 0) & (w2 - 1)) == 0)
    before = mask(before).astype(BF16)
    b = small_ref[0:receptors, 0:slots].astype(I32)
    high = (b >> 6).astype(F32).astype(BF16)
    low = (b & 63).astype(F32).astype(BF16)
    spread = nn(high, sel_s) * 64.0 + nn(low, sel_s)
    on_row = iota((receptors, cols), 0) == r_of
    geo = jnp.sum(jnp.where(on_row, spread, 0.0), axis=0, keepdims=True).astype(I32)
    place = small_ref[at_place : at_place + 1, :].astype(I32)
    row16 = iota((16, ids), 0)
    owner_tab = (place >> log2(local_blocks)).astype(F32)
    local_tab = (place & (local_blocks - 1)).astype(F32)
    tab = jnp.where(row16 == 0, owner_tab, jnp.where(row16 == 1, local_tab, 0.0)).astype(BF16)
    found = nn(tab, mask(iota((ids, cols), 0) == geo).astype(BF16))
    step = found[0:1].astype(I32) - me
    step = jnp.where(step < 0, step + n, step)
    local_row = found[1:2]
    to_owner = iota((up(n, 16), cols), 0) == step
    ranks = nn(mask(to_owner).astype(BF16), before)
    rank = jnp.sum(jnp.where(to_owner, ranks, 0.0), axis=0, keepdims=True).astype(I32)
    slot = step * capp + rank
    hour = small_ref[at_place + 1 : at_place + 2, 0:receptors]
    weight = small_ref[at_place + 2 : at_place + 3, 0:receptors]
    w_hi = weight.astype(BF16).astype(F32)
    w_mid = (weight - w_hi).astype(BF16).astype(F32)
    w_lo = weight - w_hi - w_mid
    row_r = iota((16, receptors), 0)
    per_r = jnp.where(row_r == 1, hour, 0.0)
    per_r = jnp.where(row_r == 3, w_hi, per_r)
    per_r = jnp.where(row_r == 4, w_mid, per_r)
    per_r = jnp.where(row_r == 5, w_lo, per_r)
    values = nn(per_r.astype(BF16), sel_r)
    row_m = iota((16, cols), 0)
    values = jnp.where(row_m == 0, local_row + 1.0, values)
    values = jnp.where(row_m == 1, values + (tm * w2).astype(F32), values)
    values = jnp.where(row_m == 2, (r_of + me * receptors).astype(F32), values)
    fp = fp_ref[...].reshape(cols, fp_ref.shape[2])
    for w in range(w2):
        slot_w = jnp.where(w_of == w, slot, -1)
        pick = mask(iota((padded, cols), 0) == slot_w).astype(BF16)
        moved = nn(pick, fp).astype(BF16)
        for d in range(n):
            outs[d][w * capp : (w + 1) * capp, :] = moved[d * capp : (d + 1) * capp]
        if w == 0:
            meta = nt(values.astype(BF16), pick)
            at = iota((16, half * capp), 1)
            for d in range(n):
                base = d // half * half * capp
                place_d = d % half * capp
                mine = meta[:, base : base + half * capp]
                mine = jnp.where((at >= place_d) & (at < place_d + capp), mine, 0.0).astype(BF16)
                outs[d][w2 * capp : w2 * capp + META, :] = jnp.zeros((META, outs[d].shape[1]), BF16)
                outs[d][w2 * capp : w2 * capp + META, 0 : half * capp] = mine


def pack(cfg, where, blocks, hour_start, obs_weight, placement, footprint):
    n, capp, slots, w2 = cfg["n"], cfg["capp"], cfg["slots"], cfg["w2"]
    receptors = blocks.shape[0]
    cells = footprint.shape[3]
    rows = w2 * capp + META
    ids = placement.shape[0]
    height = up(receptors + 3, 8)

    def put(x, at):
        return jnp.pad(x, ((at, height - at - x.shape[0]), (0, ids - x.shape[1])))

    small = put(blocks, 0) + put(placement[None], receptors) + put(hour_start[None], receptors + 1)
    small = small.astype(F32) + put(obs_weight[None], receptors + 2)
    vm = pl.BlockSpec(memory_space=pltpu.VMEM)
    return pl.pallas_call(
        functools.partial(pack_kernel, cfg),
        out_shape=[jax.ShapeDtypeStruct((rows, cells), BF16)] * n,
        in_specs=[pl.BlockSpec(memory_space=pltpu.SMEM), vm, vm],
        out_specs=[vm] * n,
        compiler_params=pltpu.CompilerParams(vmem_limit_bytes=VMEM_LIMIT),
        name="pack",
    )(where, small, footprint.reshape(receptors * slots, w2, cells))


def slots_of(bufs, rows):
    return [(buf, base) for buf in bufs for base in range(0, buf.shape[0], rows)]


def load_meta(cfg, placed):
    w2, capp = cfg["w2"], cfg["capp"]
    total = None
    for buf, base in placed:
        part = buf[base + w2 * capp : base + w2 * capp + META, :].astype(F32)
        total = part if total is None else total + part
    return total[:, 0 : len(placed) * capp]


def hour_column(meta, width):
    pick = mask(iota((16, width), 0) == 1)
    return lax.dot_general(
        meta.astype(BF16), pick.astype(BF16), (((0,), (0,)), ((), ())), preferred_element_type=F32
    )


def spread_hours(cfg, sides, metas, f8_ref, base_row):
    w2, capp, hours, cells = cfg["w2"], cfg["capp"], cfg["hours"], cfg["cells"]
    columns = [hour_column(m, cells).astype(BF16) for m in metas]
    for d in range(len(sides[0])):
        parts = []
        for side in range(len(sides)):
            buf, base = sides[side][d]
            first = columns[side][d * capp : (d + 1) * capp]
            for w in range(w2):
                parts.append((first + BF16(w) if w else first, buf[base + w * capp : base + (w + 1) * capp, :]))
        for h in range(hours):
            value = jnp.zeros((capp, cells), BF16)
            for first, fp in parts:
                value = jnp.where(first == BF16(h), fp, value)
            f8_ref[base_row + d * capp : base_row + (d + 1) * capp, h * cells : (h + 1) * cells] = value


def after_kernel(x_ref, unread_ref, out_ref):
    out_ref[...] = x_ref[...]


def after(x, first):
    return pl.pallas_call(
        after_kernel,
        out_shape=jax.ShapeDtypeStruct(x.shape, x.dtype),
        grid=(1,),
        in_specs=[pl.BlockSpec(x.shape, lambda i: (0, 0)), pl.BlockSpec((16, 128), lambda i: (0, 0))],
        out_specs=pl.BlockSpec(x.shape, lambda i: (0, 0)),
        compiler_params=pltpu.CompilerParams(vmem_limit_bytes=4 * 1024 * 1024),
        cost_estimate=pl.CostEstimate(flops=0, bytes_accessed=2 * x.size, transcendentals=0),
        name="after",
    )(x, first)


def stack_kernel(count, *refs):
    out_ref, at = refs[-1], 0
    for ref in refs[:count]:
        out_ref[at : at + ref.shape[0], :] = ref[...]
        at += ref.shape[0]


def stack(bufs, *unread):
    vm = pl.BlockSpec(memory_space=pltpu.VMEM)
    rows = sum(b.shape[0] for b in bufs)
    return pl.pallas_call(
        functools.partial(stack_kernel, len(bufs)),
        out_shape=jax.ShapeDtypeStruct((rows, bufs[0].shape[1]), BF16),
        in_specs=[vm] * (len(bufs) + len(unread)),
        out_specs=vm,
        compiler_params=pltpu.CompilerParams(vmem_limit_bytes=16 * 1024 * 1024),
        cost_estimate=pl.CostEstimate(flops=0, bytes_accessed=0, transcendentals=0),
        name="stack",
    )(*bufs, *unread)


def forward_kernel(cfg, counts, *refs):
    local, k, rows, capp = cfg["local"], cfg["k_core"], cfg["rows"], cfg["capp"]
    half = cfg["n"] // 2 * capp
    out_ref, f8_ref = refs[-2:]
    at = 0
    firsts = []
    for i, sides_n in enumerate(counts):
        sides = []
        for count in sides_n:
            sides.append(slots_of(refs[at : at + count], rows))
            at += count
        metas = [load_meta(cfg, placed) for placed in sides]
        spread_hours(cfg, sides, metas, f8_ref, i * half)
        firsts.append(metas[0][0:8])
    probes_ref = refs[at]
    meta = jnp.concatenate(firsts, axis=1)
    used = meta.shape[1]
    own = iota((local, used), 0) + 1 == meta[0:1].astype(I32)
    row = iota((8, used), 0)
    dots = jnp.zeros((8, used), F32)
    f8 = f8_ref[...]
    x = nt(probes_ref[...], f8)
    for j in range(k):
        y = jnp.sum(jnp.where(own, x[j * local : (j + 1) * local], 0.0), axis=0, keepdims=True)
        dots = jnp.where(row == j, y, dots)
    to_r = mask(iota((out_ref.shape[1], used), 0) == meta[2:3].astype(I32)).astype(BF16)
    out_ref[...] = add_three(nt(three(dots), to_r))


def forward(cfg, own, probes_t, out_shape, unread):
    n, capp, hours, cells = cfg["n"], cfg["capp"], cfg["hours"], cfg["cells"]
    args = [b for half in own for side in half for b in side]
    counts = [[len(side) for side in half] for half in own]
    vm = pl.BlockSpec(memory_space=pltpu.VMEM)
    return pl.pallas_call(
        functools.partial(forward_kernel, cfg, counts),
        out_shape=jax.ShapeDtypeStruct(out_shape, F32),
        in_specs=[vm] * (len(args) + 1) + [pl.BlockSpec(memory_space=pl.ANY)] * len(unread),
        out_specs=vm,
        scratch_shapes=[pltpu.VMEM((n * capp, hours * cells), BF16)],
        compiler_params=pltpu.CompilerParams(vmem_limit_bytes=VMEM_LIMIT),
        cost_estimate=pl.CostEstimate(flops=0, bytes_accessed=FORWARD_BYTES, transcendentals=0),
        name="forward",
    )(*args, probes_t, *unread)


def prepare_kernel(cfg, column, counts, *refs):
    n, capp, local = cfg["n"], cfg["capp"], cfg["local"]
    f8_ref, own_ref, to_r_ref, weight_ref = refs[-4:]
    used = n * capp
    at = 0
    whole = [[] for _ in counts[0]]
    for sides_n in counts:
        for side, count in enumerate(sides_n):
            whole[side] += slots_of(refs[at : at + count], cfg["rows"])
            at += count
    firsts = []
    for i in range(2):
        sides = [side[i * n // 2 : (i + 1) * n // 2] for side in whole]
        metas = [load_meta(cfg, placed) for placed in sides]
        spread_hours(cfg, sides, metas, f8_ref, column * used + i * (n // 2) * capp)
        firsts.append(metas[0][0:8])
    meta = jnp.concatenate(firsts, axis=1)
    lanes = slice(column * used, (column + 1) * used)
    own_ref[:, lanes] = mask(iota((local, used), 0) + 1 == meta[0:1].astype(I32)).astype(BF16)
    to_r_ref[:, lanes] = mask(iota((to_r_ref.shape[0], used), 0) == meta[2:3].astype(I32)).astype(BF16)
    weight_ref[:, lanes] = jnp.broadcast_to(meta[3:4] + meta[4:5] + meta[5:6], (8, used))


def prepare(cfg, column, halves, columns, rp, before, *unread):
    n, capp, hours, cells, local = cfg["n"], cfg["capp"], cfg["hours"], cfg["cells"], cfg["local"]
    total = columns * n * capp
    args = [b for sides in halves for side in sides for b in side]
    counts = [[len(side) for side in sides] for sides in halves]
    vm = pl.BlockSpec(memory_space=pltpu.VMEM)
    return pl.pallas_call(
        functools.partial(prepare_kernel, cfg, column, counts),
        out_shape=[
            jax.ShapeDtypeStruct((total, hours * cells), BF16),
            jax.ShapeDtypeStruct((local, total), BF16),
            jax.ShapeDtypeStruct((rp, total), BF16),
            jax.ShapeDtypeStruct((8, total), F32),
        ],
        in_specs=[vm] * (len(args) + len(before) + len(unread)),
        out_specs=[vm] * 4,
        input_output_aliases={len(args) + i: i for i in range(len(before))},
        compiler_params=pltpu.CompilerParams(vmem_limit_bytes=VMEM_LIMIT),
        cost_estimate=pl.CostEstimate(flops=0, bytes_accessed=3 * total * cells, transcendentals=0),
        name=f"prepare{column}",
    )(*args, *before, *unread)


def fill_terms(cfg, reg, obs_ref, own, to_r, weight, a_ref, lanes):
    local, kd = cfg["local"], cfg["kd"]
    used = own.shape[1]
    row = iota((8, used), 0)
    per_entry = add_three(nn(three(obs_ref[...]), to_r)) * weight
    for j in range(kd):
        term = jnp.sum(jnp.where(row == reg * kd + j, per_entry, 0.0), axis=0, keepdims=True)
        high = term.astype(BF16).astype(F32)
        for p, part in enumerate((high, term - high)):
            spread = jnp.broadcast_to(part.astype(BF16), (local, used))
            a_ref[(2 * j + p) * local : (2 * j + p + 1) * local, lanes] = own * spread


def own_adjoint_kernel(cfg, where_ref, f8_ref, own_ref, to_r_ref, weight_ref, obs_ref, out_ref, a_ref):
    local, hours, cells, kd = cfg["local"], cfg["hours"], cfg["cells"], cfg["kd"]
    fill_terms(cfg, where_ref[2], obs_ref, own_ref[...], to_r_ref[...], weight_ref[...], a_ref, slice(None))
    a = a_ref[...]
    for h in range(hours):
        sums = nn(a, f8_ref[:, h * cells : (h + 1) * cells])
        for j in range(kd):
            both = sums[2 * j * local : (2 * j + 1) * local] + sums[(2 * j + 1) * local : (2 * j + 2) * local]
            out_ref[j * local : (j + 1) * local, h * cells : (h + 1) * cells] = both


def own_adjoint(cfg, where, operands, observed):
    hours, cells, local, kd = cfg["hours"], cfg["cells"], cfg["local"], cfg["kd"]
    total = operands[0].shape[0]
    vm = pl.BlockSpec(memory_space=pltpu.VMEM)
    return pl.pallas_call(
        functools.partial(own_adjoint_kernel, cfg),
        out_shape=jax.ShapeDtypeStruct((kd * local, hours * cells), F32),
        in_specs=[pl.BlockSpec(memory_space=pltpu.SMEM)] + [vm] * 5,
        out_specs=vm,
        scratch_shapes=[pltpu.VMEM((2 * kd * local, total), BF16)],
        compiler_params=pltpu.CompilerParams(vmem_limit_bytes=VMEM_LIMIT),
        cost_estimate=pl.CostEstimate(
            flops=4 * kd * local * total * hours * cells, bytes_accessed=2 * total * hours * cells, transcendentals=0
        ),
        name="own_adjoint",
    )(where, *operands, observed)


def adjoint_kernel(cfg, where_ref, before_ref, f8_ref, own_ref, to_r_ref, weight_ref, *refs):
    n, capp, local, hours, cells, kd = (
        cfg["n"], cfg["capp"], cfg["local"], cfg["hours"], cfg["cells"], cfg["kd"],
    )
    obs_refs, (out_ref, a_ref, tiles_ref, sems) = refs[:-4], refs[-4:]
    used = n * capp
    per_k = cells // 128
    for c, obs_ref in enumerate(obs_refs):
        lanes = slice(c * used, (c + 1) * used)
        fill_terms(
            cfg, where_ref[2], obs_ref, own_ref[:, lanes], to_r_ref[:, lanes], weight_ref[:, lanes], a_ref, lanes
        )
    copies = []
    part = local // QUARTERS
    rows = part * hours
    for q in range(QUARTERS):
        a = jnp.concatenate(
            [a_ref[i * local + q * part : i * local + (q + 1) * part, :] for i in range(2 * kd)], axis=0
        )
        for h in range(hours):
            sums = nn(a, f8_ref[:, h * cells : (h + 1) * cells])
            for j in range(kd):
                both = sums[2 * j * part : (2 * j + 1) * part] + sums[(2 * j + 1) * part : (2 * j + 2) * part]
                at = j * local + q * part
                both = both + before_ref[at : at + part, h * cells : (h + 1) * cells]
                for t in range(per_k):
                    tile = tiles_ref.at[j * per_k + t]
                    tile[pl.ds(q * rows + h, part, stride=hours), :] = both[:, t * 128 : (t + 1) * 128]
        for t in range(kd * per_k):
            copy = pltpu.make_async_copy(
                tiles_ref.at[t, pl.ds(q * rows, rows)],
                out_ref.at[pl.ds(q * rows, rows), pl.ds(t * 128, 128)],
                sems.at[t, q],
            )
            copy.start()
            copies.append(copy)
    for copy in copies:
        copy.wait()


def adjoint(cfg, where, before, operands, observed):
    hours, cells, local, kd = cfg["hours"], cfg["cells"], cfg["local"], cfg["kd"]
    total = operands[0].shape[0]
    vm = pl.BlockSpec(memory_space=pltpu.VMEM)
    return pl.pallas_call(
        functools.partial(adjoint_kernel, cfg),
        out_shape=jax.ShapeDtypeStruct((local * hours, kd * cells), F32),
        in_specs=[pl.BlockSpec(memory_space=pltpu.SMEM)] + [vm] * (5 + len(observed)),
        out_specs=pl.BlockSpec(memory_space=pl.ANY),
        scratch_shapes=[
            pltpu.VMEM((2 * kd * local, total), BF16),
            pltpu.VMEM((kd * cells // 128, local * hours, 128), F32),
            pltpu.SemaphoreType.DMA((kd * cells // 128, QUARTERS)),
        ],
        compiler_params=pltpu.CompilerParams(vmem_limit_bytes=VMEM_LIMIT),
        name="adjoint",
    )(where, before, *operands, *observed)


def shift(x, axis, d):
    n = lax.axis_size(axis)
    return lax.ppermute(x, axis, [(i, (i + d) % n) for i in range(n)])


def swap(x, axis, bits):
    n = lax.axis_size(axis)
    assert n & (n - 1) == 0
    return lax.ppermute(x, axis, [(i, i ^ bits) for i in range(n)])


def shards(probes, footprint, blocks, hour_start, obs_weight, placement):
    n, nreg, ntm = lax.axis_size("rcp"), lax.axis_size("reg"), lax.axis_size("tm")
    local, hours, width = probes.shape
    receptors, slots, w2, cells = footprint.shape
    k = width // cells
    kd = k // (nreg * ntm)
    capp = up(3 * receptors * slots // (2 * n), 16)
    cfg = dict(
        n=n, capp=capp, local=local, hours=hours, cells=cells, receptors=receptors, slots=slots, w2=w2,
        kd=kd, k_core=nreg * kd, rows=w2 * capp + META,
    )
    z, reg, tm = lax.axis_index("rcp"), lax.axis_index("reg"), lax.axis_index("tm")
    where = jnp.stack([z, tm, reg]).astype(I32)
    outs = pack(cfg, where, blocks, hour_start, obs_weight, placement, footprint)
    probes_t = lax.dynamic_index_in_dim(probes.reshape(local, hours, nreg, ntm, kd, cells), tm, 3, keepdims=False)
    probes_t = probes_t.transpose(2, 3, 0, 1, 4).reshape(nreg * kd * local, hours * cells)

    def with_cores(half):
        return [half] + [[shift(b, "tm", s) for b in half] for s in range(1, ntm)]

    mine = after(outs[0], probes_t)
    bufs = [mine] + [shift(outs[d], "rcp", d) for d in range(1, n)]
    raw = [outs[0]] + bufs[1:]
    halves = [bufs[: n // 2], bufs[n // 2 :]]
    groups = GROUPS
    if n > 4:
        halves = [[jnp.concatenate(half, axis=0)] for half in halves]
        raw, groups = [half[0] for half in halves], ((0,), (1,))
    own = [with_cores(half) for half in halves]
    sent = [stack([raw[d] for d in group]) if len(group) > 1 else raw[group[0]] for group in groups]
    across = [[shift(b, "reg", g) for b in sent] for g in range(1, nreg)]
    rp = up(n * receptors, 128)
    partial = forward(cfg, own, probes_t, (8, rp), [b for group in across for b in group[:EARLY]])
    observed = partial
    for d in range(1, n):
        observed = observed + swap(partial, "rcp", d)
    operands = prepare(cfg, 0, own, 1, rp, [], partial)
    before = own_adjoint(cfg, where, operands, observed)
    gate, operands = operands[3], []
    for g, group in enumerate(across):
        group = stack(group, observed, gate)
        operands = prepare(cfg, g, [with_cores([group])], nreg - 1, rp, operands)
    observed = [shift(observed, "reg", g) for g in range(1, nreg)]
    result = adjoint(cfg, where, before, operands, observed)
    return result.reshape(local, hours, kd * cells)


def solution(mesh):
    return jax.shard_map(
        shards,
        mesh=mesh,
        in_specs=(
            P(("inv", "rcp"), None, None),
            P(("inv", "rcp", "reg"), None, "tm", None),
            P(("inv", "rcp", "reg"), None),
            P(("inv", "rcp", "reg")),
            P(("inv", "rcp", "reg")),
            P("inv"),
        ),
        out_specs=P(("inv", "rcp"), None, ("reg", "tm")),
        check_vma=False,
    )
```

```python
import functools

import jax
import jax.numpy as jnp
from jax import lax
from jax.experimental import pallas as pl
from jax.experimental.pallas import tpu as pltpu
from jax.sharding import PartitionSpec as P

F32 = jnp.float32
BF16 = jnp.bfloat16
I32 = jnp.int32
QUARTERS = 4
META = 16
VMEM_LIMIT = 48 * 1024 * 1024
GROUPS = ((0,), (1, 2, 3))
EARLY = 1
FORWARD_BYTES = 0


def up(x, m):
    return (x + m - 1) // m * m


def log2(x):
    assert x & (x - 1) == 0
    return x.bit_length() - 1


def iota(shape, axis):
    return lax.broadcasted_iota(I32, shape, axis)


def mask(cond):
    return jnp.where(cond, jnp.float32(1), jnp.float32(0))


def nt(a, b):
    return lax.dot_general(a, b, (((1,), (1,)), ((), ())), preferred_element_type=F32)


def nn(a, b):
    return lax.dot_general(a, b, (((1,), (0,)), ((), ())), preferred_element_type=F32)


def three(x):
    high = x.astype(BF16).astype(F32)
    mid = (x - high).astype(BF16).astype(F32)
    return jnp.concatenate([high, mid, x - high - mid], axis=0).astype(BF16)


def add_three(x):
    rows = x.shape[0] // 3
    return x[0:rows] + x[rows : 2 * rows] + x[2 * rows : 3 * rows]


def pack_kernel(cfg, where_ref, small_ref, fp_ref, *outs):
    n, capp, local_blocks, slots, w2 = cfg["n"], cfg["capp"], cfg["local"], cfg["slots"], cfg["w2"]
    receptors = cfg["receptors"]
    cols = receptors * slots * w2
    ids = small_ref.shape[1]
    at_place = receptors
    used = n * capp
    padded = up(used, 256)
    half = n // 2
    me = where_ref[0]
    tm = where_ref[1]
    lane = iota((1, cols), 1)
    entry = lane >> log2(w2)
    w_of = lane & (w2 - 1)
    s_of = entry & (slots - 1)
    r_of = entry >> log2(slots)
    sel_s = mask(iota((slots, cols), 0) == s_of).astype(BF16)
    sel_r = mask(iota((receptors, cols), 0) == r_of).astype(BF16)
    before = ((iota((cols, cols), 0) >> log2(w2)) < entry) & ((iota((cols, cols), 0) & (w2 - 1)) == 0)
    before = mask(before).astype(BF16)
    b = small_ref[0:receptors, 0:slots].astype(I32)
    high = (b >> 6).astype(F32).astype(BF16)
    low = (b & 63).astype(F32).astype(BF16)
    spread = nn(high, sel_s) * 64.0 + nn(low, sel_s)
    on_row = iota((receptors, cols), 0) == r_of
    geo = jnp.sum(jnp.where(on_row, spread, 0.0), axis=0, keepdims=True).astype(I32)
    place = small_ref[at_place : at_place + 1, :].astype(I32)
    row16 = iota((16, ids), 0)
    owner_tab = (place >> log2(local_blocks)).astype(F32)
    local_tab = (place & (local_blocks - 1)).astype(F32)
    tab = jnp.where(row16 == 0, owner_tab, jnp.where(row16 == 1, local_tab, 0.0)).astype(BF16)
    found = nn(tab, mask(iota((ids, cols), 0) == geo).astype(BF16))
    step = found[0:1].astype(I32) - me
    step = jnp.where(step < 0, step + n, step)
    local_row = found[1:2]
    to_owner = iota((up(n, 16), cols), 0) == step
    ranks = nn(mask(to_owner).astype(BF16), before)
    rank = jnp.sum(jnp.where(to_owner, ranks, 0.0), axis=0, keepdims=True).astype(I32)
    slot = step * capp + rank
    hour = small_ref[at_place + 1 : at_place + 2, 0:receptors]
    weight = small_ref[at_place + 2 : at_place + 3, 0:receptors]
    w_hi = weight.astype(BF16).astype(F32)
    w_mid = (weight - w_hi).astype(BF16).astype(F32)
    w_lo = weight - w_hi - w_mid
    row_r = iota((16, receptors), 0)
    per_r = jnp.where(row_r == 1, hour, 0.0)
    per_r = jnp.where(row_r == 3, w_hi, per_r)
    per_r = jnp.where(row_r == 4, w_mid, per_r)
    per_r = jnp.where(row_r == 5, w_lo, per_r)
    values = nn(per_r.astype(BF16), sel_r)
    row_m = iota((16, cols), 0)
    values = jnp.where(row_m == 0, local_row + 1.0, values)
    values = jnp.where(row_m == 1, values + (tm * w2).astype(F32), values)
    values = jnp.where(row_m == 2, (r_of + me * receptors).astype(F32), values)
    fp = fp_ref[...].reshape(cols, fp_ref.shape[2])
    for w in range(w2):
        slot_w = jnp.where(w_of == w, slot, -1)
        pick = mask(iota((padded, cols), 0) == slot_w).astype(BF16)
        moved = nn(pick, fp).astype(BF16)
        for d in range(n):
            outs[d][w * capp : (w + 1) * capp, :] = moved[d * capp : (d + 1) * capp]
        if w == 0:
            meta = nt(values.astype(BF16), pick)
            at = iota((16, half * capp), 1)
            for d in range(n):
                base = d // half * half * capp
                place_d = d % half * capp
                mine = meta[:, base : base + half * capp]
                mine = jnp.where((at >= place_d) & (at < place_d + capp), mine, 0.0).astype(BF16)
                outs[d][w2 * capp : w2 * capp + META, :] = jnp.zeros((META, outs[d].shape[1]), BF16)
                outs[d][w2 * capp : w2 * capp + META, 0 : half * capp] = mine


def pack(cfg, where, blocks, hour_start, obs_weight, placement, footprint):
    n, capp, slots, w2 = cfg["n"], cfg["capp"], cfg["slots"], cfg["w2"]
    receptors = blocks.shape[0]
    cells = footprint.shape[3]
    rows = w2 * capp + META
    ids = placement.shape[0]
    height = up(receptors + 3, 8)

    def put(x, at):
        return jnp.pad(x, ((at, height - at - x.shape[0]), (0, ids - x.shape[1])))

    small = put(blocks, 0) + put(placement[None], receptors) + put(hour_start[None], receptors + 1)
    small = small.astype(F32) + put(obs_weight[None], receptors + 2)
    vm = pl.BlockSpec(memory_space=pltpu.VMEM)
    return pl.pallas_call(
        functools.partial(pack_kernel, cfg),
        out_shape=[jax.ShapeDtypeStruct((rows, cells), BF16)] * n,
        in_specs=[pl.BlockSpec(memory_space=pltpu.SMEM), vm, vm],
        out_specs=[vm] * n,
        compiler_params=pltpu.CompilerParams(vmem_limit_bytes=VMEM_LIMIT),
        name="pack",
    )(where, small, footprint.reshape(receptors * slots, w2, cells))


def slots_of(bufs, rows):
    return [(buf, base) for buf in bufs for base in range(0, buf.shape[0], rows)]


def load_meta(cfg, placed):
    w2, capp = cfg["w2"], cfg["capp"]
    total = None
    for buf, base in placed:
        part = buf[base + w2 * capp : base + w2 * capp + META, :].astype(F32)
        total = part if total is None else total + part
    return total[:, 0 : len(placed) * capp]


def hour_column(meta, width):
    pick = mask(iota((16, width), 0) == 1)
    return lax.dot_general(
        meta.astype(BF16), pick.astype(BF16), (((0,), (0,)), ((), ())), preferred_element_type=F32
    )


def spread_hours(cfg, sides, metas, f8_ref, base_row):
    w2, capp, hours, cells = cfg["w2"], cfg["capp"], cfg["hours"], cfg["cells"]
    columns = [hour_column(m, cells).astype(BF16) for m in metas]
    for d in range(len(sides[0])):
        parts = []
        for side in range(len(sides)):
            buf, base = sides[side][d]
            first = columns[side][d * capp : (d + 1) * capp]
            for w in range(w2):
                parts.append((first + BF16(w) if w else first, buf[base + w * capp : base + (w + 1) * capp, :]))
        for h in range(hours):
            value = jnp.zeros((capp, cells), BF16)
            for first, fp in parts:
                value = jnp.where(first == BF16(h), fp, value)
            f8_ref[base_row + d * capp : base_row + (d + 1) * capp, h * cells : (h + 1) * cells] = value


def after_kernel(x_ref, unread_ref, out_ref):
    out_ref[...] = x_ref[...]


def after(x, first):
    return pl.pallas_call(
        after_kernel,
        out_shape=jax.ShapeDtypeStruct(x.shape, x.dtype),
        grid=(1,),
        in_specs=[pl.BlockSpec(x.shape, lambda i: (0, 0)), pl.BlockSpec((16, 128), lambda i: (0, 0))],
        out_specs=pl.BlockSpec(x.shape, lambda i: (0, 0)),
        compiler_params=pltpu.CompilerParams(vmem_limit_bytes=4 * 1024 * 1024),
        cost_estimate=pl.CostEstimate(flops=0, bytes_accessed=2 * x.size, transcendentals=0),
        name="after",
    )(x, first)


def stack_kernel(count, *refs):
    out_ref, at = refs[-1], 0
    for ref in refs[:count]:
        out_ref[at : at + ref.shape[0], :] = ref[...]
        at += ref.shape[0]


def stack(bufs, *unread):
    vm = pl.BlockSpec(memory_space=pltpu.VMEM)
    rows = sum(b.shape[0] for b in bufs)
    return pl.pallas_call(
        functools.partial(stack_kernel, len(bufs)),
        out_shape=jax.ShapeDtypeStruct((rows, bufs[0].shape[1]), BF16),
        in_specs=[vm] * (len(bufs) + len(unread)),
        out_specs=vm,
        compiler_params=pltpu.CompilerParams(vmem_limit_bytes=16 * 1024 * 1024),
        cost_estimate=pl.CostEstimate(flops=0, bytes_accessed=0, transcendentals=0),
        name="stack",
    )(*bufs, *unread)


def forward_kernel(cfg, counts, *refs):
    local, k, rows, capp = cfg["local"], cfg["k_core"], cfg["rows"], cfg["capp"]
    half = cfg["n"] // 2 * capp
    out_ref, f8_ref = refs[-2:]
    probes_ref = refs[sum(sum(sides_n) for sides_n in counts)]
    at = 0
    metas = []
    for i, sides_n in enumerate(counts):
        sides = []
        for count in sides_n:
            sides.append(slots_of(refs[at : at + count], rows))
            at += count
        side_metas = [load_meta(cfg, placed) for placed in sides]
        spread_hours(cfg, sides, side_metas, f8_ref, i * half)
        metas.append(side_metas[0])
    row = iota((8, half), 0)
    total = 0.0
    for i, meta in enumerate(metas):
        own = iota((local, half), 0) + 1 == meta[0:1].astype(I32)
        x = nt(probes_ref[...], f8_ref[i * half : (i + 1) * half, :])
        dots = jnp.zeros((8, half), F32)
        for j in range(k):
            y = jnp.sum(jnp.where(own, x[j * local : (j + 1) * local], 0.0), axis=0, keepdims=True)
            dots = jnp.where(row == j, y, dots)
        to_r = mask(iota((out_ref.shape[1], half), 0) == meta[2:3].astype(I32)).astype(BF16)
        total = total + add_three(nt(three(dots), to_r))
    out_ref[...] = total


def forward(cfg, own, probes_t, out_shape, unread):
    n, capp, hours, cells = cfg["n"], cfg["capp"], cfg["hours"], cfg["cells"]
    args = [b for half in own for side in half for b in side]
    counts = [[len(side) for side in half] for half in own]
    vm = pl.BlockSpec(memory_space=pltpu.VMEM)
    return pl.pallas_call(
        functools.partial(forward_kernel, cfg, counts),
        out_shape=jax.ShapeDtypeStruct(out_shape, F32),
        in_specs=[vm] * (len(args) + 1) + [pl.BlockSpec(memory_space=pl.ANY)] * len(unread),
        out_specs=vm,
        scratch_shapes=[pltpu.VMEM((n * capp, hours * cells), BF16)],
        compiler_params=pltpu.CompilerParams(vmem_limit_bytes=VMEM_LIMIT),
        cost_estimate=pl.CostEstimate(flops=0, bytes_accessed=FORWARD_BYTES, transcendentals=0),
        name="forward",
    )(*args, probes_t, *unread)


def prepare_kernel(cfg, column, counts, *refs):
    n, capp, local = cfg["n"], cfg["capp"], cfg["local"]
    f8_ref, own_ref, to_r_ref, weight_ref = refs[-4:]
    used = n * capp
    at = 0
    whole = [[] for _ in counts[0]]
    for sides_n in counts:
        for side, count in enumerate(sides_n):
            whole[side] += slots_of(refs[at : at + count], cfg["rows"])
            at += count
    firsts = []
    for i in range(2):
        sides = [side[i * n // 2 : (i + 1) * n // 2] for side in whole]
        metas = [load_meta(cfg, placed) for placed in sides]
        spread_hours(cfg, sides, metas, f8_ref, column * used + i * (n // 2) * capp)
        firsts.append(metas[0][0:8])
    meta = jnp.concatenate(firsts, axis=1)
    lanes = slice(column * used, (column + 1) * used)
    own_ref[:, lanes] = mask(iota((local, used), 0) + 1 == meta[0:1].astype(I32)).astype(BF16)
    to_r_ref[:, lanes] = mask(iota((to_r_ref.shape[0], used), 0) == meta[2:3].astype(I32)).astype(BF16)
    weight_ref[:, lanes] = jnp.broadcast_to(meta[3:4] + meta[4:5] + meta[5:6], (8, used))


def prepare(cfg, column, halves, columns, rp, before, *unread):
    n, capp, hours, cells, local = cfg["n"], cfg["capp"], cfg["hours"], cfg["cells"], cfg["local"]
    total = columns * n * capp
    args = [b for sides in halves for side in sides for b in side]
    counts = [[len(side) for side in sides] for sides in halves]
    vm = pl.BlockSpec(memory_space=pltpu.VMEM)
    return pl.pallas_call(
        functools.partial(prepare_kernel, cfg, column, counts),
        out_shape=[
            jax.ShapeDtypeStruct((total, hours * cells), BF16),
            jax.ShapeDtypeStruct((local, total), BF16),
            jax.ShapeDtypeStruct((rp, total), BF16),
            jax.ShapeDtypeStruct((8, total), F32),
        ],
        in_specs=[vm] * (len(args) + len(before) + len(unread)),
        out_specs=[vm] * 4,
        input_output_aliases={len(args) + i: i for i in range(len(before))},
        compiler_params=pltpu.CompilerParams(vmem_limit_bytes=VMEM_LIMIT),
        cost_estimate=pl.CostEstimate(flops=0, bytes_accessed=3 * total * cells, transcendentals=0),
        name=f"prepare{column}",
    )(*args, *before, *unread)


def fill_terms(cfg, reg, obs_ref, own, to_r, weight, a_ref, lanes):
    local, kd = cfg["local"], cfg["kd"]
    used = own.shape[1]
    row = iota((8, used), 0)
    per_entry = add_three(nn(three(obs_ref[...]), to_r)) * weight
    for j in range(kd):
        term = jnp.sum(jnp.where(row == reg * kd + j, per_entry, 0.0), axis=0, keepdims=True)
        high = term.astype(BF16).astype(F32)
        for p, part in enumerate((high, term - high)):
            spread = jnp.broadcast_to(part.astype(BF16), (local, used))
            a_ref[(2 * j + p) * local : (2 * j + p + 1) * local, lanes] = own * spread


def own_adjoint_kernel(cfg, where_ref, f8_ref, own_ref, to_r_ref, weight_ref, obs_ref, out_ref, a_ref):
    local, hours, cells, kd = cfg["local"], cfg["hours"], cfg["cells"], cfg["kd"]
    fill_terms(cfg, where_ref[2], obs_ref, own_ref[...], to_r_ref[...], weight_ref[...], a_ref, slice(None))
    a = a_ref[...]
    for h in range(hours):
        sums = nn(a, f8_ref[:, h * cells : (h + 1) * cells])
        for j in range(kd):
            both = sums[2 * j * local : (2 * j + 1) * local] + sums[(2 * j + 1) * local : (2 * j + 2) * local]
            out_ref[j * local : (j + 1) * local, h * cells : (h + 1) * cells] = both


def own_adjoint(cfg, where, operands, observed):
    hours, cells, local, kd = cfg["hours"], cfg["cells"], cfg["local"], cfg["kd"]
    total = operands[0].shape[0]
    vm = pl.BlockSpec(memory_space=pltpu.VMEM)
    return pl.pallas_call(
        functools.partial(own_adjoint_kernel, cfg),
        out_shape=jax.ShapeDtypeStruct((kd * local, hours * cells), F32),
        in_specs=[pl.BlockSpec(memory_space=pltpu.SMEM)] + [vm] * 5,
        out_specs=vm,
        scratch_shapes=[pltpu.VMEM((2 * kd * local, total), BF16)],
        compiler_params=pltpu.CompilerParams(vmem_limit_bytes=VMEM_LIMIT),
        cost_estimate=pl.CostEstimate(
            flops=4 * kd * local * total * hours * cells, bytes_accessed=2 * total * hours * cells, transcendentals=0
        ),
        name="own_adjoint",
    )(where, *operands, observed)


def adjoint_kernel(cfg, where_ref, before_ref, f8_ref, own_ref, to_r_ref, weight_ref, *refs):
    n, capp, local, hours, cells, kd = (
        cfg["n"], cfg["capp"], cfg["local"], cfg["hours"], cfg["cells"], cfg["kd"],
    )
    obs_refs, (out_ref, a_ref, tiles_ref, sems) = refs[:-4], refs[-4:]
    used = n * capp
    per_k = cells // 128
    for c, obs_ref in enumerate(obs_refs):
        lanes = slice(c * used, (c + 1) * used)
        fill_terms(
            cfg, where_ref[2], obs_ref, own_ref[:, lanes], to_r_ref[:, lanes], weight_ref[:, lanes], a_ref, lanes
        )
    copies = []
    part = local // QUARTERS
    rows = part * hours
    for q in range(QUARTERS):
        a = jnp.concatenate(
            [a_ref[i * local + q * part : i * local + (q + 1) * part, :] for i in range(2 * kd)], axis=0
        )
        for h in range(hours):
            sums = nn(a, f8_ref[:, h * cells : (h + 1) * cells])
            for j in range(kd):
                both = sums[2 * j * part : (2 * j + 1) * part] + sums[(2 * j + 1) * part : (2 * j + 2) * part]
                at = j * local + q * part
                both = both + before_ref[at : at + part, h * cells : (h + 1) * cells]
                for t in range(per_k):
                    tile = tiles_ref.at[j * per_k + t]
                    tile[pl.ds(q * rows + h, part, stride=hours), :] = both[:, t * 128 : (t + 1) * 128]
        for t in range(kd * per_k):
            copy = pltpu.make_async_copy(
                tiles_ref.at[t, pl.ds(q * rows, rows)],
                out_ref.at[pl.ds(q * rows, rows), pl.ds(t * 128, 128)],
                sems.at[t, q],
            )
            copy.start()
            copies.append(copy)
    for copy in copies:
        copy.wait()


def adjoint(cfg, where, before, operands, observed):
    hours, cells, local, kd = cfg["hours"], cfg["cells"], cfg["local"], cfg["kd"]
    total = operands[0].shape[0]
    vm = pl.BlockSpec(memory_space=pltpu.VMEM)
    return pl.pallas_call(
        functools.partial(adjoint_kernel, cfg),
        out_shape=jax.ShapeDtypeStruct((local * hours, kd * cells), F32),
        in_specs=[pl.BlockSpec(memory_space=pltpu.SMEM)] + [vm] * (5 + len(observed)),
        out_specs=pl.BlockSpec(memory_space=pl.ANY),
        scratch_shapes=[
            pltpu.VMEM((2 * kd * local, total), BF16),
            pltpu.VMEM((kd * cells // 128, local * hours, 128), F32),
            pltpu.SemaphoreType.DMA((kd * cells // 128, QUARTERS)),
        ],
        compiler_params=pltpu.CompilerParams(vmem_limit_bytes=VMEM_LIMIT),
        name="adjoint",
    )(where, before, *operands, *observed)


def shift(x, axis, d):
    n = lax.axis_size(axis)
    return lax.ppermute(x, axis, [(i, (i + d) % n) for i in range(n)])


def swap(x, axis, bits):
    n = lax.axis_size(axis)
    assert n & (n - 1) == 0
    return lax.ppermute(x, axis, [(i, i ^ bits) for i in range(n)])


def shards(probes, footprint, blocks, hour_start, obs_weight, placement):
    n, nreg, ntm = lax.axis_size("rcp"), lax.axis_size("reg"), lax.axis_size("tm")
    local, hours, width = probes.shape
    receptors, slots, w2, cells = footprint.shape
    k = width // cells
    kd = k // (nreg * ntm)
    capp = up(3 * receptors * slots // (2 * n), 16)
    cfg = dict(
        n=n, capp=capp, local=local, hours=hours, cells=cells, receptors=receptors, slots=slots, w2=w2,
        kd=kd, k_core=nreg * kd, rows=w2 * capp + META,
    )
    z, reg, tm = lax.axis_index("rcp"), lax.axis_index("reg"), lax.axis_index("tm")
    where = jnp.stack([z, tm, reg]).astype(I32)
    outs = pack(cfg, where, blocks, hour_start, obs_weight, placement, footprint)
    probes_t = lax.dynamic_index_in_dim(probes.reshape(local, hours, nreg, ntm, kd, cells), tm, 3, keepdims=False)
    probes_t = probes_t.transpose(2, 3, 0, 1, 4).reshape(nreg * kd * local, hours * cells)

    def with_cores(half):
        return [half] + [[shift(b, "tm", s) for b in half] for s in range(1, ntm)]

    mine = after(outs[0], probes_t)
    bufs = [mine] + [shift(outs[d], "rcp", d) for d in range(1, n)]
    raw = [outs[0]] + bufs[1:]
    halves = [bufs[: n // 2], bufs[n // 2 :]]
    groups = GROUPS
    if n > 4:
        halves = [[jnp.concatenate(half, axis=0)] for half in halves]
        raw, groups = [half[0] for half in halves], ((0,), (1,))
    own = [with_cores(half) for half in halves]
    sent = [stack([raw[d] for d in group]) if len(group) > 1 else raw[group[0]] for group in groups]
    across = [[shift(b, "reg", g) for b in sent] for g in range(1, nreg)]
    rp = up(n * receptors, 128)
    partial = forward(cfg, own, probes_t, (8, rp), [b for group in across for b in group[:EARLY]])
    observed = partial
    for d in range(1, n):
        observed = observed + swap(partial, "rcp", d)
    operands = prepare(cfg, 0, own, 1, rp, [], partial)
    before = own_adjoint(cfg, where, operands, observed)
    gate, operands = operands[3], []
    for g, group in enumerate(across):
        group = stack(group, observed, gate)
        operands = prepare(cfg, g, [with_cores([group])], nreg - 1, rp, operands)
    observed = [shift(observed, "reg", g) for g in range(1, nreg)]
    result = adjoint(cfg, where, before, operands, observed)
    return result.reshape(local, hours, kd * cells)


def solution(mesh):
    return jax.shard_map(
        shards,
        mesh=mesh,
        in_specs=(
            P(("inv", "rcp"), None, None),
            P(("inv", "rcp", "reg"), None, "tm", None),
            P(("inv", "rcp", "reg"), None),
            P(("inv", "rcp", "reg")),
            P(("inv", "rcp", "reg")),
            P("inv"),
        ),
        out_specs=P(("inv", "rcp"), None, ("reg", "tm")),
        check_vma=False,
    )
```

```python
import functools

import jax
import jax.numpy as jnp
from jax import lax
from jax.experimental import pallas as pl
from jax.experimental.pallas import tpu as pltpu
from jax.sharding import PartitionSpec as P

F32 = jnp.float32
BF16 = jnp.bfloat16
I32 = jnp.int32
QUARTERS = 4
META = 16
VMEM_LIMIT = 48 * 1024 * 1024
GROUPS = ((0,), (1, 2, 3))
EARLY = 1
FORWARD_BYTES = 0


def up(x, m):
    return (x + m - 1) // m * m


def log2(x):
    assert x & (x - 1) == 0
    return x.bit_length() - 1


def iota(shape, axis):
    return lax.broadcasted_iota(I32, shape, axis)


def mask(cond):
    return jnp.where(cond, jnp.float32(1), jnp.float32(0))


def nt(a, b):
    return lax.dot_general(a, b, (((1,), (1,)), ((), ())), preferred_element_type=F32)


def nn(a, b):
    return lax.dot_general(a, b, (((1,), (0,)), ((), ())), preferred_element_type=F32)


def three(x):
    high = x.astype(BF16).astype(F32)
    mid = (x - high).astype(BF16).astype(F32)
    return jnp.concatenate([high, mid, x - high - mid], axis=0).astype(BF16)


def add_three(x):
    rows = x.shape[0] // 3
    return x[0:rows] + x[rows : 2 * rows] + x[2 * rows : 3 * rows]


def pack_kernel(cfg, where_ref, small_ref, fp_ref, *outs):
    n, capp, local_blocks, slots, w2 = cfg["n"], cfg["capp"], cfg["local"], cfg["slots"], cfg["w2"]
    receptors = cfg["receptors"]
    cols = receptors * slots * w2
    ids = small_ref.shape[1]
    at_place = receptors
    used = n * capp
    padded = up(used, 256)
    half = n // 2
    me = where_ref[0]
    tm = where_ref[1]
    lane = iota((1, cols), 1)
    entry = lane >> log2(w2)
    w_of = lane & (w2 - 1)
    s_of = entry & (slots - 1)
    r_of = entry >> log2(slots)
    sel_s = mask(iota((slots, cols), 0) == s_of).astype(BF16)
    sel_r = mask(iota((receptors, cols), 0) == r_of).astype(BF16)
    before = ((iota((cols, cols), 0) >> log2(w2)) < entry) & ((iota((cols, cols), 0) & (w2 - 1)) == 0)
    before = mask(before).astype(BF16)
    b = small_ref[0:receptors, 0:slots].astype(I32)
    high = (b >> 6).astype(F32).astype(BF16)
    low = (b & 63).astype(F32).astype(BF16)
    spread = nn(high, sel_s) * 64.0 + nn(low, sel_s)
    on_row = iota((receptors, cols), 0) == r_of
    geo = jnp.sum(jnp.where(on_row, spread, 0.0), axis=0, keepdims=True).astype(I32)
    place = small_ref[at_place : at_place + 1, :].astype(I32)
    row16 = iota((16, ids), 0)
    owner_tab = (place >> log2(local_blocks)).astype(F32)
    local_tab = (place & (local_blocks - 1)).astype(F32)
    tab = jnp.where(row16 == 0, owner_tab, jnp.where(row16 == 1, local_tab, 0.0)).astype(BF16)
    found = nn(tab, mask(iota((ids, cols), 0) == geo).astype(BF16))
    step = found[0:1].astype(I32) - me
    step = jnp.where(step < 0, step + n, step)
    local_row = found[1:2]
    to_owner = iota((up(n, 16), cols), 0) == step
    ranks = nn(mask(to_owner).astype(BF16), before)
    rank = jnp.sum(jnp.where(to_owner, ranks, 0.0), axis=0, keepdims=True).astype(I32)
    slot = step * capp + rank
    hour = small_ref[at_place + 1 : at_place + 2, 0:receptors]
    weight = small_ref[at_place + 2 : at_place + 3, 0:receptors]
    w_hi = weight.astype(BF16).astype(F32)
    w_mid = (weight - w_hi).astype(BF16).astype(F32)
    w_lo = weight - w_hi - w_mid
    row_r = iota((16, receptors), 0)
    per_r = jnp.where(row_r == 1, hour, 0.0)
    per_r = jnp.where(row_r == 3, w_hi, per_r)
    per_r = jnp.where(row_r == 4, w_mid, per_r)
    per_r = jnp.where(row_r == 5, w_lo, per_r)
    values = nn(per_r.astype(BF16), sel_r)
    row_m = iota((16, cols), 0)
    values = jnp.where(row_m == 0, local_row + 1.0, values)
    values = jnp.where(row_m == 1, values + (tm * w2).astype(F32), values)
    values = jnp.where(row_m == 2, (r_of + me * receptors).astype(F32), values)
    fp = fp_ref[...].reshape(cols, fp_ref.shape[2])
    for w in range(w2):
        slot_w = jnp.where(w_of == w, slot, -1)
        pick = mask(iota((used if w else padded, cols), 0) == slot_w).astype(BF16)
        moved = nn(pick[0:used], fp).astype(BF16)
        for d in range(n):
            outs[d][w * capp : (w + 1) * capp, :] = moved[d * capp : (d + 1) * capp]
        if w == 0:
            meta = nt(values.astype(BF16), pick)
            at = iota((16, half * capp), 1)
            for d in range(n):
                base = d // half * half * capp
                place_d = d % half * capp
                mine = meta[:, base : base + half * capp]
                mine = jnp.where((at >= place_d) & (at < place_d + capp), mine, 0.0).astype(BF16)
                outs[d][w2 * capp : w2 * capp + META, :] = jnp.zeros((META, outs[d].shape[1]), BF16)
                outs[d][w2 * capp : w2 * capp + META, 0 : half * capp] = mine


def pack(cfg, where, blocks, hour_start, obs_weight, placement, footprint):
    n, capp, slots, w2 = cfg["n"], cfg["capp"], cfg["slots"], cfg["w2"]
    receptors = blocks.shape[0]
    cells = footprint.shape[3]
    rows = w2 * capp + META
    ids = placement.shape[0]
    height = up(receptors + 3, 8)

    def put(x, at):
        return jnp.pad(x, ((at, height - at - x.shape[0]), (0, ids - x.shape[1])))

    small = put(blocks, 0) + put(placement[None], receptors) + put(hour_start[None], receptors + 1)
    small = small.astype(F32) + put(obs_weight[None], receptors + 2)
    vm = pl.BlockSpec(memory_space=pltpu.VMEM)
    return pl.pallas_call(
        functools.partial(pack_kernel, cfg),
        out_shape=[jax.ShapeDtypeStruct((rows, cells), BF16)] * n,
        in_specs=[pl.BlockSpec(memory_space=pltpu.SMEM), vm, vm],
        out_specs=[vm] * n,
        compiler_params=pltpu.CompilerParams(vmem_limit_bytes=VMEM_LIMIT),
        name="pack",
    )(where, small, footprint.reshape(receptors * slots, w2, cells))


def slots_of(bufs, rows):
    return [(buf, base) for buf in bufs for base in range(0, buf.shape[0], rows)]


def load_meta(cfg, placed):
    w2, capp = cfg["w2"], cfg["capp"]
    total = None
    for buf, base in placed:
        part = buf[base + w2 * capp : base + w2 * capp + META, :].astype(F32)
        total = part if total is None else total + part
    return total[:, 0 : len(placed) * capp]


def hour_column(meta, width):
    pick = mask(iota((16, width), 0) == 1)
    return lax.dot_general(
        meta.astype(BF16), pick.astype(BF16), (((0,), (0,)), ((), ())), preferred_element_type=F32
    )


def spread_hours(cfg, sides, metas, f8_ref, base_row):
    w2, capp, hours, cells = cfg["w2"], cfg["capp"], cfg["hours"], cfg["cells"]
    columns = [hour_column(m, cells).astype(BF16) for m in metas]
    for d in range(len(sides[0])):
        parts = []
        for side in range(len(sides)):
            buf, base = sides[side][d]
            first = columns[side][d * capp : (d + 1) * capp]
            for w in range(w2):
                parts.append((first + BF16(w) if w else first, buf[base + w * capp : base + (w + 1) * capp, :]))
        for h in range(hours):
            value = jnp.zeros((capp, cells), BF16)
            for first, fp in parts:
                value = jnp.where(first == BF16(h), fp, value)
            f8_ref[base_row + d * capp : base_row + (d + 1) * capp, h * cells : (h + 1) * cells] = value


def after_kernel(x_ref, unread_ref, out_ref):
    out_ref[...] = x_ref[...]


def after(x, first):
    return pl.pallas_call(
        after_kernel,
        out_shape=jax.ShapeDtypeStruct(x.shape, x.dtype),
        grid=(1,),
        in_specs=[pl.BlockSpec(x.shape, lambda i: (0, 0)), pl.BlockSpec((16, 128), lambda i: (0, 0))],
        out_specs=pl.BlockSpec(x.shape, lambda i: (0, 0)),
        compiler_params=pltpu.CompilerParams(vmem_limit_bytes=4 * 1024 * 1024),
        cost_estimate=pl.CostEstimate(flops=0, bytes_accessed=2 * x.size, transcendentals=0),
        name="after",
    )(x, first)


def stack_kernel(count, *refs):
    out_ref, at = refs[-1], 0
    for ref in refs[:count]:
        out_ref[at : at + ref.shape[0], :] = ref[...]
        at += ref.shape[0]


def stack(bufs, *unread):
    vm = pl.BlockSpec(memory_space=pltpu.VMEM)
    rows = sum(b.shape[0] for b in bufs)
    return pl.pallas_call(
        functools.partial(stack_kernel, len(bufs)),
        out_shape=jax.ShapeDtypeStruct((rows, bufs[0].shape[1]), BF16),
        in_specs=[vm] * (len(bufs) + len(unread)),
        out_specs=vm,
        compiler_params=pltpu.CompilerParams(vmem_limit_bytes=16 * 1024 * 1024),
        cost_estimate=pl.CostEstimate(flops=0, bytes_accessed=0, transcendentals=0),
        name="stack",
    )(*bufs, *unread)


def forward_kernel(cfg, counts, *refs):
    local, k, rows, capp = cfg["local"], cfg["k_core"], cfg["rows"], cfg["capp"]
    half = cfg["n"] // 2 * capp
    out_ref, f8_ref = refs[-2:]
    probes_ref = refs[sum(sum(sides_n) for sides_n in counts)]
    at = 0
    metas = []
    for i, sides_n in enumerate(counts):
        sides = []
        for count in sides_n:
            sides.append(slots_of(refs[at : at + count], rows))
            at += count
        side_metas = [load_meta(cfg, placed) for placed in sides]
        spread_hours(cfg, sides, side_metas, f8_ref, i * half)
        metas.append(side_metas[0])
    row = iota((8, half), 0)
    total = 0.0
    for i, meta in enumerate(metas):
        own = iota((local, half), 0) + 1 == meta[0:1].astype(I32)
        x = nt(probes_ref[...], f8_ref[i * half : (i + 1) * half, :])
        dots = jnp.zeros((8, half), F32)
        for j in range(k):
            y = jnp.sum(jnp.where(own, x[j * local : (j + 1) * local], 0.0), axis=0, keepdims=True)
            dots = jnp.where(row == j, y, dots)
        to_r = mask(iota((out_ref.shape[1], half), 0) == meta[2:3].astype(I32)).astype(BF16)
        total = total + add_three(nt(three(dots), to_r))
    out_ref[...] = total


def forward(cfg, own, probes_t, out_shape, unread):
    n, capp, hours, cells = cfg["n"], cfg["capp"], cfg["hours"], cfg["cells"]
    args = [b for half in own for side in half for b in side]
    counts = [[len(side) for side in half] for half in own]
    vm = pl.BlockSpec(memory_space=pltpu.VMEM)
    return pl.pallas_call(
        functools.partial(forward_kernel, cfg, counts),
        out_shape=jax.ShapeDtypeStruct(out_shape, F32),
        in_specs=[vm] * (len(args) + 1) + [pl.BlockSpec(memory_space=pl.ANY)] * len(unread),
        out_specs=vm,
        scratch_shapes=[pltpu.VMEM((n * capp, hours * cells), BF16)],
        compiler_params=pltpu.CompilerParams(vmem_limit_bytes=VMEM_LIMIT),
        cost_estimate=pl.CostEstimate(flops=0, bytes_accessed=FORWARD_BYTES, transcendentals=0),
        name="forward",
    )(*args, probes_t, *unread)


def prepare_kernel(cfg, column, counts, *refs):
    n, capp, local = cfg["n"], cfg["capp"], cfg["local"]
    f8_ref, own_ref, to_r_ref, weight_ref = refs[-4:]
    used = n * capp
    at = 0
    whole = [[] for _ in counts[0]]
    for sides_n in counts:
        for side, count in enumerate(sides_n):
            whole[side] += slots_of(refs[at : at + count], cfg["rows"])
            at += count
    firsts = []
    for i in range(2):
        sides = [side[i * n // 2 : (i + 1) * n // 2] for side in whole]
        metas = [load_meta(cfg, placed) for placed in sides]
        spread_hours(cfg, sides, metas, f8_ref, column * used + i * (n // 2) * capp)
        firsts.append(metas[0][0:8])
    meta = jnp.concatenate(firsts, axis=1)
    lanes = slice(column * used, (column + 1) * used)
    own_ref[:, lanes] = mask(iota((local, used), 0) + 1 == meta[0:1].astype(I32)).astype(BF16)
    to_r_ref[:, lanes] = mask(iota((to_r_ref.shape[0], used), 0) == meta[2:3].astype(I32)).astype(BF16)
    weight_ref[:, lanes] = jnp.broadcast_to(meta[3:4] + meta[4:5] + meta[5:6], (8, used))


def prepare(cfg, column, halves, columns, rp, before, *unread):
    n, capp, hours, cells, local = cfg["n"], cfg["capp"], cfg["hours"], cfg["cells"], cfg["local"]
    total = columns * n * capp
    args = [b for sides in halves for side in sides for b in side]
    counts = [[len(side) for side in sides] for sides in halves]
    vm = pl.BlockSpec(memory_space=pltpu.VMEM)
    return pl.pallas_call(
        functools.partial(prepare_kernel, cfg, column, counts),
        out_shape=[
            jax.ShapeDtypeStruct((total, hours * cells), BF16),
            jax.ShapeDtypeStruct((local, total), BF16),
            jax.ShapeDtypeStruct((rp, total), BF16),
            jax.ShapeDtypeStruct((8, total), F32),
        ],
        in_specs=[vm] * (len(args) + len(before) + len(unread)),
        out_specs=[vm] * 4,
        input_output_aliases={len(args) + i: i for i in range(len(before))},
        compiler_params=pltpu.CompilerParams(vmem_limit_bytes=VMEM_LIMIT),
        cost_estimate=pl.CostEstimate(flops=0, bytes_accessed=3 * total * cells, transcendentals=0),
        name=f"prepare{column}",
    )(*args, *before, *unread)


def fill_terms(cfg, reg, obs_ref, own, to_r, weight, a_ref, lanes):
    local, kd = cfg["local"], cfg["kd"]
    used = own.shape[1]
    row = iota((8, used), 0)
    per_entry = add_three(nn(three(obs_ref[...]), to_r)) * weight
    for j in range(kd):
        term = jnp.sum(jnp.where(row == reg * kd + j, per_entry, 0.0), axis=0, keepdims=True)
        high = term.astype(BF16).astype(F32)
        for p, part in enumerate((high, term - high)):
            spread = jnp.broadcast_to(part.astype(BF16), (local, used))
            a_ref[(2 * j + p) * local : (2 * j + p + 1) * local, lanes] = own * spread


def own_adjoint_kernel(cfg, where_ref, f8_ref, own_ref, to_r_ref, weight_ref, obs_ref, out_ref, a_ref):
    local, hours, cells, kd = cfg["local"], cfg["hours"], cfg["cells"], cfg["kd"]
    fill_terms(cfg, where_ref[2], obs_ref, own_ref[...], to_r_ref[...], weight_ref[...], a_ref, slice(None))
    a = a_ref[...]
    for h in range(hours):
        sums = nn(a, f8_ref[:, h * cells : (h + 1) * cells])
        for j in range(kd):
            both = sums[2 * j * local : (2 * j + 1) * local] + sums[(2 * j + 1) * local : (2 * j + 2) * local]
            out_ref[j * local : (j + 1) * local, h * cells : (h + 1) * cells] = both


def own_adjoint(cfg, where, operands, observed):
    hours, cells, local, kd = cfg["hours"], cfg["cells"], cfg["local"], cfg["kd"]
    total = operands[0].shape[0]
    vm = pl.BlockSpec(memory_space=pltpu.VMEM)
    return pl.pallas_call(
        functools.partial(own_adjoint_kernel, cfg),
        out_shape=jax.ShapeDtypeStruct((kd * local, hours * cells), F32),
        in_specs=[pl.BlockSpec(memory_space=pltpu.SMEM)] + [vm] * 5,
        out_specs=vm,
        scratch_shapes=[pltpu.VMEM((2 * kd * local, total), BF16)],
        compiler_params=pltpu.CompilerParams(vmem_limit_bytes=VMEM_LIMIT),
        cost_estimate=pl.CostEstimate(
            flops=4 * kd * local * total * hours * cells, bytes_accessed=2 * total * hours * cells, transcendentals=0
        ),
        name="own_adjoint",
    )(where, *operands, observed)


def adjoint_kernel(cfg, where_ref, before_ref, f8_ref, own_ref, to_r_ref, weight_ref, *refs):
    n, capp, local, hours, cells, kd = (
        cfg["n"], cfg["capp"], cfg["local"], cfg["hours"], cfg["cells"], cfg["kd"],
    )
    obs_refs, (out_ref, a_ref, tiles_ref, sems) = refs[:-4], refs[-4:]
    used = n * capp
    per_k = cells // 128
    for c, obs_ref in enumerate(obs_refs):
        lanes = slice(c * used, (c + 1) * used)
        fill_terms(
            cfg, where_ref[2], obs_ref, own_ref[:, lanes], to_r_ref[:, lanes], weight_ref[:, lanes], a_ref, lanes
        )
    copies = []
    part = local // QUARTERS
    rows = part * hours
    for q in range(QUARTERS):
        a = jnp.concatenate(
            [a_ref[i * local + q * part : i * local + (q + 1) * part, :] for i in range(2 * kd)], axis=0
        )
        for h in range(hours):
            sums = nn(a, f8_ref[:, h * cells : (h + 1) * cells])
            for j in range(kd):
                both = sums[2 * j * part : (2 * j + 1) * part] + sums[(2 * j + 1) * part : (2 * j + 2) * part]
                at = j * local + q * part
                both = both + before_ref[at : at + part, h * cells : (h + 1) * cells]
                for t in range(per_k):
                    tile = tiles_ref.at[j * per_k + t]
                    tile[pl.ds(q * rows + h, part, stride=hours), :] = both[:, t * 128 : (t + 1) * 128]
        for t in range(kd * per_k):
            copy = pltpu.make_async_copy(
                tiles_ref.at[t, pl.ds(q * rows, rows)],
                out_ref.at[pl.ds(q * rows, rows), pl.ds(t * 128, 128)],
                sems.at[t, q],
            )
            copy.start()
            copies.append(copy)
    for copy in copies:
        copy.wait()


def adjoint(cfg, where, before, operands, observed):
    hours, cells, local, kd = cfg["hours"], cfg["cells"], cfg["local"], cfg["kd"]
    total = operands[0].shape[0]
    vm = pl.BlockSpec(memory_space=pltpu.VMEM)
    return pl.pallas_call(
        functools.partial(adjoint_kernel, cfg),
        out_shape=jax.ShapeDtypeStruct((local * hours, kd * cells), F32),
        in_specs=[pl.BlockSpec(memory_space=pltpu.SMEM)] + [vm] * (5 + len(observed)),
        out_specs=pl.BlockSpec(memory_space=pl.ANY),
        scratch_shapes=[
            pltpu.VMEM((2 * kd * local, total), BF16),
            pltpu.VMEM((kd * cells // 128, local * hours, 128), F32),
            pltpu.SemaphoreType.DMA((kd * cells // 128, QUARTERS)),
        ],
        compiler_params=pltpu.CompilerParams(vmem_limit_bytes=VMEM_LIMIT),
        name="adjoint",
    )(where, before, *operands, *observed)


def shift(x, axis, d):
    n = lax.axis_size(axis)
    return lax.ppermute(x, axis, [(i, (i + d) % n) for i in range(n)])


def swap(x, axis, bits):
    n = lax.axis_size(axis)
    assert n & (n - 1) == 0
    return lax.ppermute(x, axis, [(i, i ^ bits) for i in range(n)])


def shards(probes, footprint, blocks, hour_start, obs_weight, placement):
    n, nreg, ntm = lax.axis_size("rcp"), lax.axis_size("reg"), lax.axis_size("tm")
    local, hours, width = probes.shape
    receptors, slots, w2, cells = footprint.shape
    k = width // cells
    kd = k // (nreg * ntm)
    capp = up(3 * receptors * slots // (2 * n), 16)
    cfg = dict(
        n=n, capp=capp, local=local, hours=hours, cells=cells, receptors=receptors, slots=slots, w2=w2,
        kd=kd, k_core=nreg * kd, rows=w2 * capp + META,
    )
    z, reg, tm = lax.axis_index("rcp"), lax.axis_index("reg"), lax.axis_index("tm")
    where = jnp.stack([z, tm, reg]).astype(I32)
    outs = pack(cfg, where, blocks, hour_start, obs_weight, placement, footprint)
    probes_t = lax.dynamic_index_in_dim(probes.reshape(local, hours, nreg, ntm, kd, cells), tm, 3, keepdims=False)
    probes_t = probes_t.transpose(2, 3, 0, 1, 4).reshape(nreg * kd * local, hours * cells)

    def with_cores(half):
        return [half] + [[shift(b, "tm", s) for b in half] for s in range(1, ntm)]

    mine = after(outs[0], probes_t)
    bufs = [mine] + [shift(outs[d], "rcp", d) for d in range(1, n)]
    raw = [outs[0]] + bufs[1:]
    halves = [bufs[: n // 2], bufs[n // 2 :]]
    groups = GROUPS
    if n > 4:
        halves = [[jnp.concatenate(half, axis=0)] for half in halves]
        raw, groups = [half[0] for half in halves], ((0,), (1,))
    own = [with_cores(half) for half in halves]
    sent = [stack([raw[d] for d in group]) if len(group) > 1 else raw[group[0]] for group in groups]
    across = [[shift(b, "reg", g) for b in sent] for g in range(1, nreg)]
    rp = up(n * receptors, 128)
    partial = forward(cfg, own, probes_t, (8, rp), [b for group in across for b in group[:EARLY]])
    observed = partial
    for d in range(1, n):
        observed = observed + swap(partial, "rcp", d)
    operands = prepare(cfg, 0, own, 1, rp, [], partial)
    before = own_adjoint(cfg, where, operands, observed)
    gate, operands = operands[3], []
    for g, group in enumerate(across):
        group = stack(group, observed, gate)
        operands = prepare(cfg, g, [with_cores([group])], nreg - 1, rp, operands)
    observed = [shift(observed, "reg", g) for g in range(1, nreg)]
    result = adjoint(cfg, where, before, operands, observed)
    return result.reshape(local, hours, kd * cells)


def solution(mesh):
    return jax.shard_map(
        shards,
        mesh=mesh,
        in_specs=(
            P(("inv", "rcp"), None, None),
            P(("inv", "rcp", "reg"), None, "tm", None),
            P(("inv", "rcp", "reg"), None),
            P(("inv", "rcp", "reg")),
            P(("inv", "rcp", "reg")),
            P("inv"),
        ),
        out_specs=P(("inv", "rcp"), None, ("reg", "tm")),
        check_vma=False,
    )
```

```python
import functools

import jax
import jax.numpy as jnp
from jax import lax
from jax.experimental import pallas as pl
from jax.experimental.pallas import tpu as pltpu
from jax.sharding import PartitionSpec as P

F32 = jnp.float32
BF16 = jnp.bfloat16
I32 = jnp.int32
QUARTERS = 4
META = 16
VMEM_LIMIT = 48 * 1024 * 1024
GROUPS = ((0,), (1, 2, 3))
EARLY = 1
FORWARD_BYTES = 0


def up(x, m):
    return (x + m - 1) // m * m


def log2(x):
    assert x & (x - 1) == 0
    return x.bit_length() - 1


def iota(shape, axis):
    return lax.broadcasted_iota(I32, shape, axis)


def mask(cond):
    return jnp.where(cond, jnp.float32(1), jnp.float32(0))


def nt(a, b):
    return lax.dot_general(a, b, (((1,), (1,)), ((), ())), preferred_element_type=F32)


def nn(a, b):
    return lax.dot_general(a, b, (((1,), (0,)), ((), ())), preferred_element_type=F32)


def three(x):
    high = x.astype(BF16).astype(F32)
    mid = (x - high).astype(BF16).astype(F32)
    return jnp.concatenate([high, mid, x - high - mid], axis=0).astype(BF16)


def add_three(x):
    rows = x.shape[0] // 3
    return x[0:rows] + x[rows : 2 * rows] + x[2 * rows : 3 * rows]


def pack_kernel(cfg, where_ref, small_ref, fp_ref, *outs):
    n, capp, local_blocks, slots, w2 = cfg["n"], cfg["capp"], cfg["local"], cfg["slots"], cfg["w2"]
    receptors = cfg["receptors"]
    cols = receptors * slots * w2
    ids = small_ref.shape[1]
    at_place = receptors
    used = n * capp
    padded = up(used, 256)
    half = n // 2
    me = where_ref[0]
    tm = where_ref[1]
    lane = iota((1, cols), 1)
    entry = lane >> log2(w2)
    w_of = lane & (w2 - 1)
    s_of = entry & (slots - 1)
    r_of = entry >> log2(slots)
    sel_s = mask(iota((slots, cols), 0) == s_of).astype(BF16)
    sel_r = mask(iota((receptors, cols), 0) == r_of).astype(BF16)
    before = ((iota((cols, cols), 0) >> log2(w2)) < entry) & ((iota((cols, cols), 0) & (w2 - 1)) == 0)
    before = mask(before).astype(BF16)
    b = small_ref[0:receptors, 0:slots].astype(I32)
    high = (b >> 6).astype(F32).astype(BF16)
    low = (b & 63).astype(F32).astype(BF16)
    spread = nn(high, sel_s) * 64.0 + nn(low, sel_s)
    on_row = iota((receptors, cols), 0) == r_of
    geo = jnp.sum(jnp.where(on_row, spread, 0.0), axis=0, keepdims=True).astype(I32)
    place = small_ref[at_place : at_place + 1, :].astype(I32)
    row16 = iota((16, ids), 0)
    owner_tab = (place >> log2(local_blocks)).astype(F32)
    local_tab = (place & (local_blocks - 1)).astype(F32)
    tab = jnp.where(row16 == 0, owner_tab, jnp.where(row16 == 1, local_tab, 0.0)).astype(BF16)
    found = nn(tab, mask(iota((ids, cols), 0) == geo).astype(BF16))
    step = found[0:1].astype(I32) - me
    step = jnp.where(step < 0, step + n, step)
    local_row = found[1:2]
    to_owner = iota((up(n, 16), cols), 0) == step
    ranks = nn(mask(to_owner).astype(BF16), before)
    rank = jnp.sum(jnp.where(to_owner, ranks, 0.0), axis=0, keepdims=True).astype(I32)
    slot = step * capp + rank
    hour = small_ref[at_place + 1 : at_place + 2, 0:receptors]
    weight = small_ref[at_place + 2 : at_place + 3, 0:receptors]
    w_hi = weight.astype(BF16).astype(F32)
    w_mid = (weight - w_hi).astype(BF16).astype(F32)
    w_lo = weight - w_hi - w_mid
    row_r = iota((16, receptors), 0)
    per_r = jnp.where(row_r == 1, hour, 0.0)
    per_r = jnp.where(row_r == 3, w_hi, per_r)
    per_r = jnp.where(row_r == 4, w_mid, per_r)
    per_r = jnp.where(row_r == 5, w_lo, per_r)
    values = nn(per_r.astype(BF16), sel_r)
    row_m = iota((16, cols), 0)
    values = jnp.where(row_m == 0, local_row + 1.0, values)
    values = jnp.where(row_m == 1, values + (tm * w2).astype(F32), values)
    values = jnp.where(row_m == 2, (r_of + me * receptors).astype(F32), values)
    fp = fp_ref[...].reshape(cols, fp_ref.shape[2])
    for w in range(w2):
        slot_w = jnp.where(w_of == w, slot, -1)
        pick = mask(iota((used if w else padded, cols), 0) == slot_w).astype(BF16)
        moved = nn(pick[0:used], fp).astype(BF16)
        for d in range(n):
            outs[d][w * capp : (w + 1) * capp, :] = moved[d * capp : (d + 1) * capp]
        if w == 0:
            meta = nt(values.astype(BF16), pick)
            at = iota((16, half * capp), 1)
            for d in range(n):
                base = d // half * half * capp
                place_d = d % half * capp
                mine = meta[:, base : base + half * capp]
                mine = jnp.where((at >= place_d) & (at < place_d + capp), mine, 0.0).astype(BF16)
                outs[d][w2 * capp : w2 * capp + META, :] = jnp.zeros((META, outs[d].shape[1]), BF16)
                outs[d][w2 * capp : w2 * capp + META, 0 : half * capp] = mine


def pack(cfg, where, blocks, hour_start, obs_weight, placement, footprint):
    n, capp, slots, w2 = cfg["n"], cfg["capp"], cfg["slots"], cfg["w2"]
    receptors = blocks.shape[0]
    cells = footprint.shape[3]
    rows = w2 * capp + META
    ids = placement.shape[0]
    height = up(receptors + 3, 8)

    def put(x, at):
        return jnp.pad(x, ((at, height - at - x.shape[0]), (0, ids - x.shape[1])))

    small = put(blocks, 0) + put(placement[None], receptors) + put(hour_start[None], receptors + 1)
    small = small.astype(F32) + put(obs_weight[None], receptors + 2)
    vm = pl.BlockSpec(memory_space=pltpu.VMEM)
    return pl.pallas_call(
        functools.partial(pack_kernel, cfg),
        out_shape=[jax.ShapeDtypeStruct((rows, cells), BF16)] * n,
        in_specs=[pl.BlockSpec(memory_space=pltpu.SMEM), vm, vm],
        out_specs=[vm] * n,
        compiler_params=pltpu.CompilerParams(vmem_limit_bytes=VMEM_LIMIT),
        name="pack",
    )(where, small, footprint.reshape(receptors * slots, w2, cells))


def slots_of(bufs, rows):
    return [(buf, base) for buf in bufs for base in range(0, buf.shape[0], rows)]


def load_meta(cfg, placed):
    w2, capp = cfg["w2"], cfg["capp"]
    total = None
    for buf, base in placed:
        part = buf[base + w2 * capp : base + w2 * capp + META, :].astype(F32)
        total = part if total is None else total + part
    return total[:, 0 : len(placed) * capp]


def hour_column(meta, width):
    pick = mask(iota((16, width), 0) == 1)
    return lax.dot_general(
        meta.astype(BF16), pick.astype(BF16), (((0,), (0,)), ((), ())), preferred_element_type=F32
    )


def spread_hours(cfg, sides, metas, f8_ref, base_row):
    w2, capp, hours, cells = cfg["w2"], cfg["capp"], cfg["hours"], cfg["cells"]
    columns = [hour_column(m, cells).astype(BF16) for m in metas]
    for d in range(len(sides[0])):
        parts = []
        for side in range(len(sides)):
            buf, base = sides[side][d]
            first = columns[side][d * capp : (d + 1) * capp]
            for w in range(w2):
                parts.append((first + BF16(w) if w else first, buf[base + w * capp : base + (w + 1) * capp, :]))
        for h in range(hours):
            value = jnp.zeros((capp, cells), BF16)
            for first, fp in parts:
                value = jnp.where(first == BF16(h), fp, value)
            f8_ref[base_row + d * capp : base_row + (d + 1) * capp, h * cells : (h + 1) * cells] = value


def after_kernel(x_ref, unread_ref, out_ref):
    out_ref[...] = x_ref[...]


def after(x, first):
    return pl.pallas_call(
        after_kernel,
        out_shape=jax.ShapeDtypeStruct(x.shape, x.dtype),
        grid=(1,),
        in_specs=[pl.BlockSpec(x.shape, lambda i: (0, 0)), pl.BlockSpec((16, 128), lambda i: (0, 0))],
        out_specs=pl.BlockSpec(x.shape, lambda i: (0, 0)),
        compiler_params=pltpu.CompilerParams(vmem_limit_bytes=4 * 1024 * 1024),
        cost_estimate=pl.CostEstimate(flops=0, bytes_accessed=2 * x.size, transcendentals=0),
        name="after",
    )(x, first)


def stack_kernel(count, *refs):
    out_ref, at = refs[-1], 0
    for ref in refs[:count]:
        out_ref[at : at + ref.shape[0], :] = ref[...]
        at += ref.shape[0]


def stack(bufs, *unread):
    vm = pl.BlockSpec(memory_space=pltpu.VMEM)
    rows = sum(b.shape[0] for b in bufs)
    return pl.pallas_call(
        functools.partial(stack_kernel, len(bufs)),
        out_shape=jax.ShapeDtypeStruct((rows, bufs[0].shape[1]), BF16),
        in_specs=[vm] * (len(bufs) + len(unread)),
        out_specs=vm,
        compiler_params=pltpu.CompilerParams(vmem_limit_bytes=16 * 1024 * 1024),
        cost_estimate=pl.CostEstimate(flops=0, bytes_accessed=0, transcendentals=0),
        name="stack",
    )(*bufs, *unread)


def forward_kernel(cfg, counts, *refs):
    local, k, rows, capp = cfg["local"], cfg["k_core"], cfg["rows"], cfg["capp"]
    half = cfg["n"] // 2 * capp
    out_ref, f8_ref = refs[-2:]
    probes_ref = refs[sum(sum(sides_n) for sides_n in counts)]
    at = 0
    metas = []
    for i, sides_n in enumerate(counts):
        sides = []
        for count in sides_n:
            sides.append(slots_of(refs[at : at + count], rows))
            at += count
        side_metas = [load_meta(cfg, placed) for placed in sides]
        spread_hours(cfg, sides, side_metas, f8_ref, i * half)
        metas.append(side_metas[0])
    row = iota((8, half), 0)
    total = 0.0
    for i, meta in enumerate(metas):
        own = iota((local, half), 0) + 1 == meta[0:1].astype(I32)
        x = nt(probes_ref[...], f8_ref[i * half : (i + 1) * half, :])
        dots = jnp.zeros((8, half), F32)
        for j in range(k):
            y = jnp.sum(jnp.where(own, x[j * local : (j + 1) * local], 0.0), axis=0, keepdims=True)
            dots = jnp.where(row == j, y, dots)
        to_r = mask(iota((out_ref.shape[1], half), 0) == meta[2:3].astype(I32)).astype(BF16)
        total = total + add_three(nt(three(dots), to_r))
    out_ref[...] = total


def forward(cfg, own, probes_t, out_shape, unread):
    n, capp, hours, cells = cfg["n"], cfg["capp"], cfg["hours"], cfg["cells"]
    args = [b for half in own for side in half for b in side]
    counts = [[len(side) for side in half] for half in own]
    vm = pl.BlockSpec(memory_space=pltpu.VMEM)
    return pl.pallas_call(
        functools.partial(forward_kernel, cfg, counts),
        out_shape=jax.ShapeDtypeStruct(out_shape, F32),
        in_specs=[vm] * (len(args) + 1) + [pl.BlockSpec(memory_space=pl.ANY)] * len(unread),
        out_specs=vm,
        scratch_shapes=[pltpu.VMEM((n * capp, hours * cells), BF16)],
        compiler_params=pltpu.CompilerParams(vmem_limit_bytes=VMEM_LIMIT),
        cost_estimate=pl.CostEstimate(flops=0, bytes_accessed=FORWARD_BYTES, transcendentals=0),
        name="forward",
    )(*args, probes_t, *unread)


def prepare_kernel(cfg, column, counts, *refs):
    n, capp, local = cfg["n"], cfg["capp"], cfg["local"]
    f8_ref, own_ref, to_r_ref, weight_ref = refs[-4:]
    used = n * capp
    at = 0
    whole = [[] for _ in counts[0]]
    for sides_n in counts:
        for side, count in enumerate(sides_n):
            whole[side] += slots_of(refs[at : at + count], cfg["rows"])
            at += count
    firsts = []
    for i in range(2):
        sides = [side[i * n // 2 : (i + 1) * n // 2] for side in whole]
        metas = [load_meta(cfg, placed) for placed in sides]
        spread_hours(cfg, sides, metas, f8_ref, column * used + i * (n // 2) * capp)
        firsts.append(metas[0][0:8])
    meta = jnp.concatenate(firsts, axis=1)
    lanes = slice(column * used, (column + 1) * used)
    own_ref[:, lanes] = mask(iota((local, used), 0) + 1 == meta[0:1].astype(I32)).astype(BF16)
    to_r_ref[:, lanes] = mask(iota((to_r_ref.shape[0], used), 0) == meta[2:3].astype(I32)).astype(BF16)
    weight_ref[:, lanes] = jnp.broadcast_to(meta[3:4] + meta[4:5] + meta[5:6], (8, used))


def prepare(cfg, column, halves, columns, rp, before, *unread):
    n, capp, hours, cells, local = cfg["n"], cfg["capp"], cfg["hours"], cfg["cells"], cfg["local"]
    total = columns * n * capp
    args = [b for sides in halves for side in sides for b in side]
    counts = [[len(side) for side in sides] for sides in halves]
    vm = pl.BlockSpec(memory_space=pltpu.VMEM)
    return pl.pallas_call(
        functools.partial(prepare_kernel, cfg, column, counts),
        out_shape=[
            jax.ShapeDtypeStruct((total, hours * cells), BF16),
            jax.ShapeDtypeStruct((local, total), BF16),
            jax.ShapeDtypeStruct((rp, total), BF16),
            jax.ShapeDtypeStruct((8, total), F32),
        ],
        in_specs=[vm] * (len(args) + len(before) + len(unread)),
        out_specs=[vm] * 4,
        input_output_aliases={len(args) + i: i for i in range(len(before))},
        compiler_params=pltpu.CompilerParams(vmem_limit_bytes=VMEM_LIMIT),
        cost_estimate=pl.CostEstimate(flops=0, bytes_accessed=3 * total * cells, transcendentals=0),
        name=f"prepare{column}",
    )(*args, *before, *unread)


def fill_terms(cfg, reg, obs_ref, own, to_r, weight, a_ref, lanes):
    local, kd = cfg["local"], cfg["kd"]
    used = own.shape[1]
    row = iota((8, used), 0)
    per_entry = add_three(nn(three(obs_ref[...]), to_r)) * weight
    for j in range(kd):
        term = jnp.sum(jnp.where(row == reg * kd + j, per_entry, 0.0), axis=0, keepdims=True)
        high = term.astype(BF16).astype(F32)
        for p, part in enumerate((high, term - high)):
            spread = jnp.broadcast_to(part.astype(BF16), (local, used))
            a_ref[(2 * j + p) * local : (2 * j + p + 1) * local, lanes] = own * spread


def own_adjoint_kernel(cfg, where_ref, f8_ref, own_ref, to_r_ref, weight_ref, obs_ref, out_ref, a_ref):
    local, hours, cells, kd = cfg["local"], cfg["hours"], cfg["cells"], cfg["kd"]
    fill_terms(cfg, where_ref[2], obs_ref, own_ref[...], to_r_ref[...], weight_ref[...], a_ref, slice(None))
    a = a_ref[...]
    for h in range(hours):
        sums = nn(a, f8_ref[:, h * cells : (h + 1) * cells])
        for j in range(kd):
            both = sums[2 * j * local : (2 * j + 1) * local] + sums[(2 * j + 1) * local : (2 * j + 2) * local]
            out_ref[j * local : (j + 1) * local, h * cells : (h + 1) * cells] = both


def own_adjoint(cfg, where, operands, observed):
    hours, cells, local, kd = cfg["hours"], cfg["cells"], cfg["local"], cfg["kd"]
    total = operands[0].shape[0]
    vm = pl.BlockSpec(memory_space=pltpu.VMEM)
    return pl.pallas_call(
        functools.partial(own_adjoint_kernel, cfg),
        out_shape=jax.ShapeDtypeStruct((kd * local, hours * cells), F32),
        in_specs=[pl.BlockSpec(memory_space=pltpu.SMEM)] + [vm] * 5,
        out_specs=vm,
        scratch_shapes=[pltpu.VMEM((2 * kd * local, total), BF16)],
        compiler_params=pltpu.CompilerParams(vmem_limit_bytes=VMEM_LIMIT),
        cost_estimate=pl.CostEstimate(
            flops=4 * kd * local * total * hours * cells, bytes_accessed=2 * total * hours * cells, transcendentals=0
        ),
        name="own_adjoint",
    )(where, *operands, observed)


def adjoint_kernel(cfg, where_ref, before_ref, f8_ref, own_ref, to_r_ref, weight_ref, *refs):
    n, capp, local, hours, cells, kd = (
        cfg["n"], cfg["capp"], cfg["local"], cfg["hours"], cfg["cells"], cfg["kd"],
    )
    obs_refs, (out_ref, a_ref, tiles_ref, sems) = refs[:-4], refs[-4:]
    used = n * capp
    per_k = cells // 128
    for c, obs_ref in enumerate(obs_refs):
        lanes = slice(c * used, (c + 1) * used)
        fill_terms(
            cfg, where_ref[2], obs_ref, own_ref[:, lanes], to_r_ref[:, lanes], weight_ref[:, lanes], a_ref, lanes
        )
    copies = []
    part = local // QUARTERS
    rows = part * hours
    for q in range(QUARTERS):
        a = jnp.concatenate(
            [a_ref[i * local + q * part : i * local + (q + 1) * part, :] for i in range(2 * kd)], axis=0
        )
        for h in range(hours):
            sums = nn(a, f8_ref[:, h * cells : (h + 1) * cells])
            for j in range(kd):
                both = sums[2 * j * part : (2 * j + 1) * part] + sums[(2 * j + 1) * part : (2 * j + 2) * part]
                at = j * local + q * part
                both = both + before_ref[at : at + part, h * cells : (h + 1) * cells]
                for t in range(per_k):
                    tile = tiles_ref.at[j * per_k + t]
                    tile[pl.ds(q * rows + h, part, stride=hours), :] = both[:, t * 128 : (t + 1) * 128]
        for t in range(kd * per_k):
            copy = pltpu.make_async_copy(
                tiles_ref.at[t, pl.ds(q * rows, rows)],
                out_ref.at[pl.ds(q * rows, rows), pl.ds(t * 128, 128)],
                sems.at[t, q],
            )
            copy.start()
            copies.append(copy)
    for copy in copies:
        copy.wait()


def adjoint(cfg, where, before, operands, observed):
    hours, cells, local, kd = cfg["hours"], cfg["cells"], cfg["local"], cfg["kd"]
    total = operands[0].shape[0]
    vm = pl.BlockSpec(memory_space=pltpu.VMEM)
    return pl.pallas_call(
        functools.partial(adjoint_kernel, cfg),
        out_shape=jax.ShapeDtypeStruct((local * hours, kd * cells), F32),
        in_specs=[pl.BlockSpec(memory_space=pltpu.SMEM)] + [vm] * (5 + len(observed)),
        out_specs=pl.BlockSpec(memory_space=pl.ANY),
        scratch_shapes=[
            pltpu.VMEM((2 * kd * local, total), BF16),
            pltpu.VMEM((kd * cells // 128, local * hours, 128), F32),
            pltpu.SemaphoreType.DMA((kd * cells // 128, QUARTERS)),
        ],
        compiler_params=pltpu.CompilerParams(vmem_limit_bytes=VMEM_LIMIT),
        name="adjoint",
    )(where, before, *operands, *observed)


def shift(x, axis, d):
    n = lax.axis_size(axis)
    return lax.ppermute(x, axis, [(i, (i + d) % n) for i in range(n)])


def swap(x, axis, bits):
    n = lax.axis_size(axis)
    assert n & (n - 1) == 0
    return lax.ppermute(x, axis, [(i, i ^ bits) for i in range(n)])


def shards(probes, footprint, blocks, hour_start, obs_weight, placement):
    n, nreg, ntm = lax.axis_size("rcp"), lax.axis_size("reg"), lax.axis_size("tm")
    local, hours, width = probes.shape
    receptors, slots, w2, cells = footprint.shape
    k = width // cells
    kd = k // (nreg * ntm)
    capp = up(3 * receptors * slots // (2 * n), 16)
    cfg = dict(
        n=n, capp=capp, local=local, hours=hours, cells=cells, receptors=receptors, slots=slots, w2=w2,
        kd=kd, k_core=nreg * kd, rows=w2 * capp + META,
    )
    z, reg, tm = lax.axis_index("rcp"), lax.axis_index("reg"), lax.axis_index("tm")
    where = jnp.stack([z, tm, reg]).astype(I32)
    outs = pack(cfg, where, blocks, hour_start, obs_weight, placement, footprint)
    probes_t = lax.dynamic_index_in_dim(probes.reshape(local, hours, nreg, ntm, kd, cells), tm, 3, keepdims=False)
    probes_t = probes_t.transpose(2, 3, 0, 1, 4).reshape(nreg * kd * local, hours * cells)

    def with_cores(half):
        return [half] + [[shift(b, "tm", s) for b in half] for s in range(1, ntm)]

    mine = after(outs[0], probes_t)
    bufs = [mine] + [shift(outs[d], "rcp", d) for d in range(1, n)]
    raw = [outs[0]] + bufs[1:]
    halves = [bufs[: n // 2], bufs[n // 2 :]]
    groups = GROUPS
    if n > 4:
        halves = [[jnp.concatenate(half, axis=0)] for half in halves]
        raw, groups = [half[0] for half in halves], ((0,), (1,))
    own = [with_cores(half) for half in halves]
    sent = [stack([raw[d] for d in group]) if len(group) > 1 else raw[group[0]] for group in groups]
    across = [[shift(b, "reg", g) for b in sent] for g in range(1, nreg)]
    rp = up(n * receptors, 128)
    partial = forward(cfg, own, probes_t, (8, rp), [b for group in across for b in group[:EARLY]])
    observed = partial
    for d in (2, 1, *range(3, n)):
        observed = observed + swap(partial, "rcp", d)
    operands = prepare(cfg, 0, own, 1, rp, [], partial)
    before = own_adjoint(cfg, where, operands, observed)
    gate, operands = operands[3], []
    for g, group in enumerate(across):
        group = stack(group, observed, gate)
        operands = prepare(cfg, g, [with_cores([group])], nreg - 1, rp, operands)
    observed = [shift(observed, "reg", g) for g in range(1, nreg)]
    result = adjoint(cfg, where, before, operands, observed)
    return result.reshape(local, hours, kd * cells)


def solution(mesh):
    return jax.shard_map(
        shards,
        mesh=mesh,
        in_specs=(
            P(("inv", "rcp"), None, None),
            P(("inv", "rcp", "reg"), None, "tm", None),
            P(("inv", "rcp", "reg"), None),
            P(("inv", "rcp", "reg")),
            P(("inv", "rcp", "reg")),
            P("inv"),
        ),
        out_specs=P(("inv", "rcp"), None, ("reg", "tm")),
        check_vma=False,
    )
```
